256 devices in a mesh: inner: 32 (over z_lo, y, core), outer: 8 (over x, z_hi).
Axes of the slice: x: 4, y: 4, z: 8 (z_hi: 2, z_lo: 4; z = z_hi * 4 + z_lo), core: 2. Of those that a mesh axis runs over, the one named last changes fastest.
Arguments:
- samples: float32 [2, 256, 262144], P(None, ('inner', 'outer')), may hold values from -6 to 6
- gram_index: int32 [8388608], P(('inner', 'outer')), may hold values from 0 to 7, as said below
- gram_offset: int32 [8388608], P(('inner', 'outer')), may hold values from 0 to 31
Outputs:
- z_field: float32 [67108864], P(('inner', 'outer'))
- gram_values: float32 [8388608], P(('inner', 'outer'))
The draws below stay inside these ranges and needn't reach their ends.
Inputs may be any that keep to these rules, and one draw needn't show every extreme that they name: `gram_index`: A device's first Gram point has 0 and its last 7.
All inputs are finite; a program needn't handle non-finite values.
Results may differ from the reference program's by a relative error of at most 0.00007.
Values sent between devices are 32-bit elements; how exact they have to be, the bound alone decides.
No kernel may reach another device: no remote copies, remote signals or barrier semaphores. Data moves between devices by JAX's collectives and lax.ppermute only.
A program may use at most 256 MiB of HBM per device.

```python
import jax
import jax.numpy as jnp

SEG_DEV = 262144
GAP = 8
HALF = 16
UPS = 32
LENGTH = 67108864
GRAM_DEV = 32768
GRAMS = 8388608
DEVICES = 256


def draw_gram_index(key, part):
    device_rows = GRAMS // GRAM_DEV
    jitter = jax.random.randint(key, (device_rows, GRAM_DEV), 0, GAP)
    column = jnp.arange(GRAM_DEV, dtype=jnp.int32)[None, :]
    jitter = jnp.where(column == 0, 0, jitter)
    jitter = jnp.where(column == GRAM_DEV - 1, GAP - 1, jitter)
    return jitter.reshape(GRAMS).astype(jnp.int32)


def with_ends(result, key, smallest, largest):
    dims = result.shape
    spot = [jax.random.randint(jax.random.fold_in(key, axis), (), 0, dims[axis]) for axis in range(len(dims))]
    result = result.at[tuple(spot)].set(smallest)
    longest = dims.index(max(dims))
    spot[longest] = (spot[longest] + 1) % dims[longest]
    return result.at[tuple(spot)].set(largest)


def level_of(key, shape, shards, least, largest):
    def one(position, parts):
        draws = jax.random.uniform(jax.random.fold_in(jax.random.fold_in(key, 6), position), (parts,), jnp.float32, least / len(shards), largest / len(shards))
        return jnp.repeat(jnp.exp(draws), shape[position] // parts).reshape((-1,) + (1,) * (len(shape) - position - 1))

    gain = one(*shards[0])
    for cut in shards[1:]:
        gain = gain * one(*cut)
    return gain


def normal_values(rng, dims, deviation, limit, split=(), kind=jnp.bfloat16):
    level = level_of(rng, dims, split, -0.22, 0.18) if split else 1.0
    drawn = jax.random.normal(rng, dims, jnp.float32) * deviation * level
    return jnp.minimum(jnp.maximum(drawn, -limit), limit).astype(kind)


def setup_inputs(seed: int = 0) -> dict:
    key_list = jax.random.split(jax.random.key(seed), 4)
    return {
        "samples": normal_values(key_list[0], (2, DEVICES, SEG_DEV), 1.0, 6.0, ((1, 256),), jnp.float32),
        "gram_index": draw_gram_index(jax.random.fold_in(key_list[3], 71), 0),
        "gram_offset": with_ends(jax.random.randint(key_list[2], (GRAMS,), 0, UPS), jax.random.fold_in(key_list[2], 1), 0, UPS - 1).astype(jnp.int32),
    }


deconv_rate = 4.0


def window_weight(distance):
    spread = HALF / 2.0
    return jnp.sinc(distance) * jnp.exp(-distance * distance / (2.0 * spread * spread))


def reference(samples, gram_index, gram_offset):
    signal = jnp.transpose(samples, (0, 2, 1)).reshape(2, LENGTH)
    spectrum = jnp.fft.fft(signal[0] + 1j * signal[1])
    index_k = jnp.arange(LENGTH, dtype=jnp.int32)
    centred = (index_k // SEG_DEV).astype(jnp.float32) / DEVICES + (index_k % SEG_DEV).astype(jnp.float32) / LENGTH - 0.5
    z_field = jnp.real(spectrum).astype(jnp.float32) * (LENGTH ** -0.5) * jnp.exp(deconv_rate * centred * centred)
    padded = jnp.pad(z_field, HALF)
    point_ids = jnp.arange(GRAMS, dtype=jnp.int32)
    anchor = (point_ids // GRAM_DEV) * SEG_DEV + (point_ids % GRAM_DEV) * GAP + gram_index.astype(jnp.int32) + HALF
    fraction = gram_offset.astype(jnp.float32) / UPS
    gram_values = jnp.zeros((GRAMS,), jnp.float32)
    for offset in range(1 - HALF, HALF + 1):
        gram_values = gram_values + padded[anchor + offset] * window_weight(fraction - offset)
    return z_field, gram_values
```

```python
import functools
import math

import jax
import jax.numpy as jnp
import numpy as np
from jax import lax
from jax.experimental import pallas as pl
from jax.experimental.pallas import tpu as pltpu
from jax.sharding import PartitionSpec as P

GAP = 8
HALF = 16
UPS = 32
RATE = 4.0
SPREAD = HALF / 2.0
SIDE = 512
LANES = 128
AXES = ("inner", "outer")
F32 = jnp.float32
BF16 = jnp.bfloat16
MIB = 1 << 20


def halves(table):
    high = table.astype(jnp.bfloat16)
    low = (table - high.astype(np.float64)).astype(jnp.bfloat16)
    return np.stack([high, low])


def segment_tables():
    sample = np.arange(LANES)
    tables = []
    for g in range(4):
        angle = 2.0 * np.pi * ((4 * sample[:, None] + g) * sample[None, :] % SIDE) / SIDE
        cos, sin = np.cos(angle), np.sin(angle)
        tables.append(np.block([[cos, sin], [-sin, cos]]))
    return halves(np.stack(tables))


def twiddle_table():
    u = np.arange(SIDE).reshape(LANES, 4).T.reshape(SIDE)
    c = np.arange(SIDE)
    angle = -2.0 * np.pi * (u[:, None] * c[None, :]) / (SIDE * SIDE)
    return np.stack([np.cos(angle), np.sin(angle)]).astype(np.float32)


def device_table(devices):
    n = np.arange(devices)
    angle = 2.0 * np.pi * (n[:, None] * n[None, :] % devices) / devices
    return halves(np.concatenate([np.cos(angle), np.sin(angle)], axis=1))


def split(x):
    high = x.astype(BF16)
    return high, (x - high.astype(F32)).astype(BF16)


def dot(a, b, dims):
    return lax.dot_general(a, b, (dims, ((), ())), preferred_element_type=F32)


def dot3(a, b, dims=((1,), (0,))):
    (a_high, a_low), (b_high, b_low) = a, b
    return dot(a_high, b_high, dims) + (dot(a_high, b_low, dims) + dot(a_low, b_high, dims))


def quarter(parts):
    (r0, i0), (r1, i1), (r2, i2), (r3, i3) = parts
    ar, ai, br, bi = r0 + r2, i0 + i2, r0 - r2, i0 - i2
    cr, ci, er, ei = r1 + r3, i1 + i3, r1 - r3, i1 - i3
    return [(ar + cr, ai + ci), (br + ei, bi - er), (ar - cr, ai - ci), (br - ei, bi + er)]


def times(a, b):
    return a[0] * b[0] - a[1] * b[1], a[0] * b[1] + a[1] * b[0]


def segment_kernel(devices, place_ref, x_ref, table_ref, twiddle_ref, out_ref, first_ref, second_ref):
    place = place_ref[0]
    length = SIDE * SIDE * devices
    for j in range(4):
        grid = [
            tuple(x_ref[part, pl.ds(SIDE * i + j, LANES, stride=4), :] for part in range(2))
            for i in range(4)
        ]
        for g, pair in enumerate(quarter(grid)):
            for part in range(2):
                high, low = split(pair[part])
                rows, cols = pl.ds(LANES * part, LANES), pl.ds(LANES * j, LANES)
                first_ref[0, g, rows, cols] = high
                first_ref[1, g, rows, cols] = low
    for g in range(4):
        done = dot3((table_ref[0, g], table_ref[1, g]), (first_ref[0, g], first_ref[1, g]))
        u = 4 * lax.broadcasted_iota(jnp.int32, (LANES, LANES), 0) + g
        angle = (place * u).astype(F32) * (-2.0 * math.pi / length)
        square = angle * angle
        turn = (
            1.0 - square * (0.5 - square * (1.0 / 24.0)),
            angle * (1.0 - square * (1.0 / 6.0 - square * (1.0 / 120.0))),
        )
        rows = pl.ds(LANES * g, LANES)
        grid = []
        for j in range(4):
            cols = slice(LANES * j, LANES * (j + 1))
            both = times((twiddle_ref[0, rows, cols], twiddle_ref[1, rows, cols]), turn)
            grid.append(times((done[:LANES, cols], done[LANES:, cols]), both))
        for h, pair in enumerate(quarter(grid)):
            for part in range(2):
                high, low = split(pair[part])
                cols = pl.ds(LANES * part, LANES)
                second_ref[0, h, rows, cols] = high
                second_ref[1, h, rows, cols] = low
    for h in range(4):
        done = dot3(
            (second_ref[0, h], second_ref[1, h]), (table_ref[0, h], table_ref[1, h]), ((1,), (1,))
        )
        v = 4 * lax.broadcasted_iota(jnp.int32, (8, LANES), 1) + h
        angle = (place * v).astype(F32) * (-2.0 * math.pi * SIDE / length)
        turn = (jnp.cos(angle)[:1], jnp.sin(angle)[:1])
        pair = times((done[:, :LANES], done[:, LANES:]), turn)
        for part in range(2):
            for upper in range(2):
                out_ref[pl.ds(8 * part + 4 * upper + h, SIDE // 2, stride=16), :] = pair[part][
                    SIDE // 2 * upper : SIDE // 2 * (upper + 1)
                ]


def device_kernel(devices, x_ref, table_ref, out_ref):
    for block in range(4):
        columns = []
        for e in (2 * block, 2 * block + 1):
            columns.append(
                jnp.concatenate(
                    [x_ref[pl.ds(8 * part + e, devices, stride=16), :] for part in range(2)], axis=0
                )
            )
        x = jnp.concatenate(columns, axis=1)
        done = dot3((table_ref[0], table_ref[1]), split(x))
        for i, e in enumerate((2 * block, 2 * block + 1)):
            out_ref[pl.ds(e, devices, stride=8), :] = done[:, LANES * i : LANES * (i + 1)]


def gain(devices, place, position):
    length = SIDE * SIDE * devices
    centred = place.astype(F32) / devices + position.astype(F32) / length - 0.5
    return length ** (-0.5) * jnp.exp(RATE * centred * centred)


def gram_kernel(devices, place_ref, x_ref, index_ref, offset_ref, z_ref, gram_ref, zs, ids, offs, sums):
    place = place_ref[0]
    pad = HALF
    t = lax.broadcasted_iota(jnp.int32, (LANES, LANES), 0)
    lane = lax.broadcasted_iota(jnp.int32, (LANES, LANES), 1)
    for h in range(4):
        for g in range(4):
            start = 8 * LANES * (g % 2) + 4 * (g // 2) + h
            raw = x_ref[pl.ds(start, LANES, stride=8), :]
            position = SIDE * (4 * lane + h) + 4 * t + g
            zs[h, pl.ds(pad + g, LANES, stride=4), :] = raw * gain(devices, place, position)
        for block in range(4):
            z_ref[pl.ds(4 * h + block, LANES, stride=16), :] = zs[
                h, pl.ds(pad + LANES * block, LANES), :
            ].T
    edge = lane[:pad]
    for h in range(4):
        before = zs[(h - 1) % 4, pl.ds(SIDE, pad), :]
        after = zs[(h + 1) % 4, pl.ds(pad, pad), :]
        if h == 0:
            before = jnp.where(edge == 0, 0.0, pltpu.roll(before, 1, 1))
        if h == 3:
            after = jnp.where(edge == LANES - 1, 0.0, pltpu.roll(after, LANES - 1, 1))
        zs[h, pl.ds(0, pad), :] = before
        zs[h, pl.ds(pad + SIDE, pad), :] = after
    for odd in range(2):
        ids[odd] = index_ref[pl.ds(odd, LANES, stride=2), :].T
        offs[odd] = offset_ref[pl.ds(odd, LANES, stride=2), :].T
    for h in range(4):

        def body(step, carry, h=h):
            rows = pl.ds(pl.multiple_of(64 * (h % 2) + 8 * step, 8), 8)
            index = ids[h // 2, rows, :]
            fraction = offs[h // 2, rows, :].astype(F32) * (1.0 / UPS)
            taps = [
                zs[h, pl.ds(pad + o + 64 * step, 8, stride=8), :]
                for o in range(1 - HALF, HALF + GAP)
            ]
            for bit in (2, 1, 0):
                size = 1 << bit
                chosen = (index >> bit & 1) == 1
                taps = [jnp.where(chosen, b, a) for a, b in zip(taps[:-size], taps[size:])]
            sums[h // 2, rows, :] = weighted(taps, fraction)
            return carry

        lax.fori_loop(0, 8, body, 0)
    for odd in range(2):
        gram_ref[pl.ds(odd, LANES, stride=2), :] = sums[odd].T


def weighted(taps, fraction):
    near = jnp.exp(fraction * fraction * (-0.5 / (SPREAD * SPREAD)))
    sine = jnp.sin(math.pi * fraction) * (near / math.pi)
    up = jnp.exp(fraction * (1.0 / (SPREAD * SPREAD)))
    down = jnp.exp(fraction * (-1.0 / (SPREAD * SPREAD)))
    square = fraction * fraction
    ups, downs = up, down
    total = None
    for w in range(1, HALF + 1):
        scale = (-1.0) ** w * math.exp(-0.5 * w * w / (SPREAD * SPREAD))
        term = (ups * taps[HALF - 1 + w]) * (fraction + w)
        if w < HALF:
            term = term + (downs * taps[HALF - 1 - w]) * (fraction - w)
        term = term * (scale / (square - w * w))
        total = term if total is None else total + term
        ups, downs = ups * up, downs * down
    at_zero = fraction == 0.0
    middle = jnp.where(at_zero, 1.0, sine / jnp.where(at_zero, 1.0, fraction))
    return sine * total + middle * taps[HALF - 1]


def weight(distance):
    at_zero = distance == 0.0
    safe = jnp.where(at_zero, 1.0, distance)
    sinc = jnp.where(at_zero, 1.0, jnp.sin(math.pi * safe) / (math.pi * safe))
    return sinc * jnp.exp(-0.5 * distance * distance / (SPREAD * SPREAD))


def call(kernel, out_shape, smem, count, scratch=(), flops=0, out_count=1):
    vmem = pl.BlockSpec(memory_space=pltpu.VMEM)
    first = [pl.BlockSpec(memory_space=pltpu.SMEM)] * smem
    return pl.pallas_call(
        kernel,
        out_shape=out_shape,
        in_specs=first + [vmem] * count,
        out_specs=vmem if out_count == 1 else (vmem,) * out_count,
        scratch_shapes=list(scratch),
        compiler_params=pltpu.CompilerParams(vmem_limit_bytes=48 * MIB),
        cost_estimate=pl.CostEstimate(flops=flops, bytes_accessed=4 * MIB, transcendentals=0),
    )


def segment_transform(devices, place, samples):
    points = samples.size // 2
    return call(
        functools.partial(segment_kernel, devices),
        jax.ShapeDtypeStruct((points * 2 // LANES, LANES), F32),
        1,
        3,
        [pltpu.VMEM((2, 4, 2 * LANES, SIDE), BF16), pltpu.VMEM((2, 4, SIDE, 2 * LANES), BF16)],
        3 * 2 * 8 * SIDE * SIDE * LANES,
    )(place, samples, jnp.asarray(segment_tables()), jnp.asarray(twiddle_table()))


def device_transform(devices, received):
    return call(
        functools.partial(device_kernel, devices),
        jax.ShapeDtypeStruct((received.shape[0] // 2, LANES), F32),
        0,
        2,
        (),
        3 * 2 * 2 * devices * received.shape[0] // 2 * LANES,
    )(received, jnp.asarray(device_table(devices)))


def interpolate(devices, place, timed, index, offset):
    return call(
        functools.partial(gram_kernel, devices),
        (jax.ShapeDtypeStruct(timed.shape, F32), jax.ShapeDtypeStruct(index.shape, F32)),
        1,
        3,
        [
            pltpu.VMEM((4, SIDE + 2 * HALF, LANES), F32),
            pltpu.VMEM((2, LANES, LANES), jnp.int32),
            pltpu.VMEM((2, LANES, LANES), jnp.int32),
            pltpu.VMEM((2, LANES, LANES), F32),
        ],
        1 << 26,
        2,
    )(place, timed, index, offset)


def ends(devices, place, timed):
    grid = timed.reshape(2, LANES, 2, 4, LANES)
    count = HALF // 4
    first = jnp.transpose(grid[:, :count, :, 0, 0], (1, 2, 0)).reshape(HALF)
    last = jnp.transpose(grid[:, LANES - count :, :, 3, LANES - 1], (1, 2, 0)).reshape(HALF)
    spot = jnp.arange(HALF, dtype=jnp.int32)
    return (
        first * gain(devices, place, spot),
        last * gain(devices, place, spot + SIDE * SIDE - HALF),
    )


def from_ends(before, after, index, offset):
    points = 2
    count = index.shape[0]
    spot = jnp.arange(HALF, dtype=jnp.int32)[None, :]
    j = jnp.arange(points, dtype=jnp.int32)

    def part(halo, ids, anchor, place):
        tap = place - (anchor + index[ids])[:, None]
        held = (tap > -HALF) & (tap <= HALF)
        distance = (offset[ids].astype(F32) / UPS)[:, None] - tap.astype(F32)
        return jnp.sum(jnp.where(held, halo[None, :] * weight(distance), 0.0), axis=1)

    head = part(before, slice(0, points), GAP * j, spot - HALF)
    tail = part(
        after, slice(count - points, count), GAP * (j + count - points), spot + GAP * count
    )
    return head, tail


def local(samples, gram_index, gram_offset):
    inner, outer = lax.axis_size("inner"), lax.axis_size("outer")
    devices = inner * outer
    place = (lax.axis_index("inner") * outer + lax.axis_index("outer")).astype(jnp.int32)
    spot = place.reshape(1)
    points = samples.shape[2]
    parts = segment_transform(devices, spot, samples.reshape(2, points // LANES, LANES))
    received = lax.all_to_all(parts.reshape(devices, 16, LANES), AXES, 0, 0, tiled=True)
    real = device_transform(devices, received.reshape(16 * devices, LANES))
    timed = lax.all_to_all(real.reshape(devices, 8, LANES), AXES, 0, 0, tiled=True)
    timed = timed.reshape(8 * devices, LANES)
    first, last = ends(devices, place, timed)
    up = [(i, i + 1) for i in range(devices - 1)]
    before = lax.ppermute(last, AXES, up)
    after = lax.ppermute(first, AXES, [(j, i) for i, j in up])
    rows = gram_index.shape[0] // LANES
    z_field, gram = interpolate(
        devices, spot, timed, gram_index.reshape(rows, LANES), gram_offset.reshape(rows, LANES)
    )
    gram = gram.reshape(-1)
    head, tail = from_ends(before, after, gram_index, gram_offset)
    gram = gram.at[: head.shape[0]].add(head).at[gram.shape[0] - tail.shape[0] :].add(tail)
    return z_field.reshape(points), gram


def solution(mesh):
    return jax.shard_map(
        local,
        mesh=mesh,
        in_specs=(P(None, AXES, None), P(AXES), P(AXES)),
        out_specs=(P(AXES), P(AXES)),
        check_vma=False,
    )
```

```python
import functools
import math

import jax
import jax.numpy as jnp
import numpy as np
from jax import lax
from jax.experimental import pallas as pl
from jax.experimental.pallas import tpu as pltpu
from jax.sharding import PartitionSpec as P

GAP = 8
HALF = 16
UPS = 32
RATE = 4.0
SPREAD = HALF / 2.0
SIDE = 512
LANES = 128
AXES = ("inner", "outer")
F32 = jnp.float32
BF16 = jnp.bfloat16
MIB = 1 << 20


def halves(table):
    high = table.astype(jnp.bfloat16)
    low = (table - high.astype(np.float64)).astype(jnp.bfloat16)
    return np.stack([high, low])


def segment_tables():
    sample = np.arange(LANES)
    tables = []
    for g in range(4):
        angle = 2.0 * np.pi * ((4 * sample[:, None] + g) * sample[None, :] % SIDE) / SIDE
        cos, sin = np.cos(angle), np.sin(angle)
        tables.append(np.block([[cos, sin], [-sin, cos]]))
    return halves(np.stack(tables))


def twiddle_table():
    u = np.arange(SIDE).reshape(LANES, 4).T.reshape(SIDE)
    c = np.arange(SIDE)
    angle = -2.0 * np.pi * (u[:, None] * c[None, :]) / (SIDE * SIDE)
    return np.stack([np.cos(angle), np.sin(angle)]).astype(np.float32)


def device_table(devices):
    n = np.arange(devices)
    angle = 2.0 * np.pi * (n[:, None] * n[None, :] % devices) / devices
    return halves(np.concatenate([np.cos(angle), np.sin(angle)], axis=1))


def split(x):
    high = x.astype(BF16)
    return high, (x - high.astype(F32)).astype(BF16)


def dot(a, b, dims):
    return lax.dot_general(a, b, (dims, ((), ())), preferred_element_type=F32)


def dot3(a, b, dims=((1,), (0,))):
    (a_high, a_low), (b_high, b_low) = a, b
    return dot(a_high, b_high, dims) + (dot(a_high, b_low, dims) + dot(a_low, b_high, dims))


def quarter(parts):
    (r0, i0), (r1, i1), (r2, i2), (r3, i3) = parts
    ar, ai, br, bi = r0 + r2, i0 + i2, r0 - r2, i0 - i2
    cr, ci, er, ei = r1 + r3, i1 + i3, r1 - r3, i1 - i3
    return [(ar + cr, ai + ci), (br + ei, bi - er), (ar - cr, ai - ci), (br - ei, bi + er)]


def times(a, b):
    return a[0] * b[0] - a[1] * b[1], a[0] * b[1] + a[1] * b[0]


def segment_kernel(
    devices, place_ref, x_hbm, table_hbm, twiddle_hbm, out_ref,
    x_ref, table_ref, twiddle_ref, first_ref, second_ref, sems,
):
    place = place_ref[0]
    length = SIDE * SIDE * devices
    loads = []
    for part in range(2):
        for i in range(4):
            rows = pl.ds(SIDE * i, SIDE)
            loads.append((x_hbm.at[part, rows], x_ref.at[part, rows]))
    loads.append((table_hbm, table_ref))
    for g in range(4):
        rows = pl.ds(LANES * g, LANES)
        loads.append((twiddle_hbm.at[:, rows], twiddle_ref.at[:, rows]))
    copies = [
        pltpu.make_async_copy(source, target, sems.at[k]) for k, (source, target) in enumerate(loads)
    ]
    for copy in copies:
        copy.start()
    for copy in copies[:8]:
        copy.wait()
    for j in range(4):
        grid = [
            tuple(x_ref[part, pl.ds(SIDE * i + j, LANES, stride=4), :] for part in range(2))
            for i in range(4)
        ]
        for g, pair in enumerate(quarter(grid)):
            for part in range(2):
                high, low = split(pair[part])
                rows, cols = pl.ds(LANES * part, LANES), pl.ds(LANES * j, LANES)
                first_ref[0, g, rows, cols] = high
                first_ref[1, g, rows, cols] = low
    copies[8].wait()
    for g in range(4):
        done = dot3((table_ref[0, g], table_ref[1, g]), (first_ref[0, g], first_ref[1, g]))
        u = 4 * lax.broadcasted_iota(jnp.int32, (LANES, LANES), 0) + g
        angle = (place * u).astype(F32) * (-2.0 * math.pi / length)
        square = angle * angle
        turn = (
            1.0 - square * (0.5 - square * (1.0 / 24.0)),
            angle * (1.0 - square * (1.0 / 6.0 - square * (1.0 / 120.0))),
        )
        rows = pl.ds(LANES * g, LANES)
        grid = []
        copies[9 + g].wait()
        for j in range(4):
            cols = slice(LANES * j, LANES * (j + 1))
            both = times((twiddle_ref[0, rows, cols], twiddle_ref[1, rows, cols]), turn)
            grid.append(times((done[:LANES, cols], done[LANES:, cols]), both))
        for h, pair in enumerate(quarter(grid)):
            for part in range(2):
                high, low = split(pair[part])
                cols = pl.ds(LANES * part, LANES)
                second_ref[0, h, rows, cols] = high
                second_ref[1, h, rows, cols] = low
    for h in range(4):
        done = dot3(
            (second_ref[0, h], second_ref[1, h]), (table_ref[0, h], table_ref[1, h]), ((1,), (1,))
        )
        v = 4 * lax.broadcasted_iota(jnp.int32, (8, LANES), 1) + h
        angle = (place * v).astype(F32) * (-2.0 * math.pi * SIDE / length)
        turn = (jnp.cos(angle)[:1], jnp.sin(angle)[:1])
        pair = times((done[:, :LANES], done[:, LANES:]), turn)
        for part in range(2):
            for upper in range(2):
                out_ref[pl.ds(8 * part + 4 * upper + h, SIDE // 2, stride=16), :] = pair[part][
                    SIDE // 2 * upper : SIDE // 2 * (upper + 1)
                ]


def device_kernel(devices, x_ref, table_ref, out_ref):
    for block in range(4):
        columns = []
        for e in (2 * block, 2 * block + 1):
            columns.append(
                jnp.concatenate(
                    [x_ref[pl.ds(8 * part + e, devices, stride=16), :] for part in range(2)], axis=0
                )
            )
        x = jnp.concatenate(columns, axis=1)
        done = dot3((table_ref[0], table_ref[1]), split(x))
        for i, e in enumerate((2 * block, 2 * block + 1)):
            out_ref[pl.ds(e, devices, stride=8), :] = done[:, LANES * i : LANES * (i + 1)]


def gain(devices, place, position):
    length = SIDE * SIDE * devices
    centred = place.astype(F32) / devices + position.astype(F32) / length - 0.5
    return length ** (-0.5) * jnp.exp(RATE * centred * centred)


def gram_tables_kernel(devices, place_ref, index_ref, offset_ref, gain_ref, ids_ref, weights_ref):
    place = place_ref[0]
    t = lax.broadcasted_iota(jnp.int32, (LANES, LANES), 0)
    lane = lax.broadcasted_iota(jnp.int32, (LANES, LANES), 1)
    for h in range(4):
        for g in range(4):
            position = SIDE * (4 * lane + h) + 4 * t + g
            gain_ref[h, g] = gain(devices, place, position)
    for odd in range(2):
        ids_ref[odd] = index_ref[pl.ds(odd, LANES, stride=2), :].T
        fraction = offset_ref[pl.ds(odd, LANES, stride=2), :].T.astype(F32) * (1.0 / UPS)
        put_weights(weights_ref, odd, fraction)


def put_weights(weights_ref, odd, fraction):
    near = jnp.exp(fraction * fraction * (-0.5 / (SPREAD * SPREAD)))
    sine = jnp.sin(math.pi * fraction) * (near / math.pi)
    up = jnp.exp(fraction * (1.0 / (SPREAD * SPREAD)))
    down = jnp.exp(fraction * (-1.0 / (SPREAD * SPREAD)))
    square = fraction * fraction
    ups, downs = sine * up, sine * down
    for w in range(1, HALF + 1):
        scale = (-1.0) ** w * math.exp(-0.5 * w * w / (SPREAD * SPREAD))
        share = scale / (square - w * w)
        weights_ref[HALF - 1 + w, odd] = ups * ((fraction + w) * share)
        if w < HALF:
            weights_ref[HALF - 1 - w, odd] = downs * ((fraction - w) * share)
        ups, downs = ups * up, downs * down
    at_zero = fraction == 0.0
    weights_ref[HALF - 1, odd] = jnp.where(at_zero, 1.0, sine / jnp.where(at_zero, 1.0, fraction))


def ends_kernel(x_ref, gain_ref, first_ref, last_ref):
    count = HALF // 4
    for g in range(4):
        for h, t, out_ref in ((0, 0, first_ref), (3, LANES - count, last_ref)):
            start = 8 * LANES * (g % 2) + 4 * (g // 2) + h
            low = t - t % 8
            raw = x_ref[pl.ds(start + 8 * low, 8, stride=8), :] * gain_ref[h, g, pl.ds(low, 8), :]
            out_ref[pl.ds(g, count, stride=4), :] = raw[t - low : t - low + count]


def times_kernel(x_ref, gain_ref, z_ref, held_ref):
    for h in range(4):
        for g in range(4):
            start = 8 * LANES * (g % 2) + 4 * (g // 2) + h
            raw = x_ref[pl.ds(start, LANES, stride=8), :]
            held_ref[h, pl.ds(g, LANES, stride=4), :] = raw * gain_ref[h, g]
        for block in range(4):
            z_ref[pl.ds(4 * h + block, LANES, stride=16), :] = held_ref[
                h, pl.ds(LANES * block, LANES), :
            ].T


def gram_kernel(before_ref, after_ref, held_ref, ids_ref, weights_ref, gram_ref, zs_ref, sums):
    pad = HALF
    edge = lax.broadcasted_iota(jnp.int32, (pad, LANES), 1)
    for h in range(4):
        before = held_ref[(h - 1) % 4, pl.ds(SIDE - pad, pad), :]
        after = held_ref[(h + 1) % 4, pl.ds(0, pad), :]
        if h == 0:
            before = jnp.where(edge == 0, pltpu.roll(before_ref[...], 1, 1), pltpu.roll(before, 1, 1))
        if h == 3:
            after = jnp.where(
                edge == LANES - 1,
                pltpu.roll(after_ref[...], LANES - 1, 1),
                pltpu.roll(after, LANES - 1, 1),
            )
        zs_ref[h, pl.ds(0, pad), :] = before
        zs_ref[h, pl.ds(pad, SIDE), :] = held_ref[h]
        zs_ref[h, pl.ds(pad + SIDE, pad), :] = after
    for h in range(4):

        def body(step, carry, h=h):
            rows = pl.ds(pl.multiple_of(64 * (h % 2) + 8 * step, 8), 8)
            index = ids_ref[h // 2, rows, :]
            taps = [
                zs_ref[h, pl.ds(pad + o + 64 * step, 8, stride=8), :]
                for o in range(1 - HALF, HALF + GAP)
            ]
            for bit in (2, 1, 0):
                size = 1 << bit
                chosen = (index >> bit & 1) == 1
                taps = [jnp.where(chosen, b, a) for a, b in zip(taps[:-size], taps[size:])]
            terms = [tap * weights_ref[w, h // 2, rows, :] for w, tap in enumerate(taps)]
            while len(terms) > 1:
                terms = [a + b for a, b in zip(terms[::2], terms[1::2])]
            sums[h // 2, rows, :] = terms[0]
            return carry

        lax.fori_loop(0, 8, body, 0)
    for odd in range(2):
        gram_ref[pl.ds(odd, LANES, stride=2), :] = sums[odd].T


def call(kernel, out_shape, specs, scratch=(), flops=0):
    spaces = {"s": pltpu.SMEM, "v": pltpu.VMEM, "h": pltpu.HBM}
    vmem = pl.BlockSpec(memory_space=pltpu.VMEM)
    return pl.pallas_call(
        kernel,
        out_shape=out_shape,
        in_specs=[pl.BlockSpec(memory_space=spaces[spec]) for spec in specs],
        out_specs=jax.tree.map(lambda shape: vmem, out_shape),
        scratch_shapes=list(scratch),
        compiler_params=pltpu.CompilerParams(vmem_limit_bytes=40 * MIB),
        cost_estimate=pl.CostEstimate(flops=flops, bytes_accessed=4 * MIB, transcendentals=0),
    )


def struct(shape, kind=F32):
    return jax.ShapeDtypeStruct(tuple(shape), kind)


def segment_transform(devices, place, samples):
    points = samples.size // 2
    table, twiddle = segment_tables(), twiddle_table()
    return call(
        functools.partial(segment_kernel, devices),
        struct((points * 2 // LANES, LANES)),
        "shhh",
        [
            pltpu.VMEM(samples.shape, F32),
            pltpu.VMEM(table.shape, BF16),
            pltpu.VMEM(twiddle.shape, F32),
            pltpu.VMEM((2, 4, 2 * LANES, SIDE), BF16),
            pltpu.VMEM((2, 4, SIDE, 2 * LANES), BF16),
            pltpu.SemaphoreType.DMA((13,)),
        ],
        3 * 2 * 8 * SIDE * SIDE * LANES,
    )(place, samples, jnp.asarray(table), jnp.asarray(twiddle))


def device_transform(devices, received):
    return call(
        functools.partial(device_kernel, devices),
        struct((received.shape[0] // 2, LANES)),
        "vv",
        flops=3 * 2 * 2 * devices * received.shape[0] // 2 * LANES,
    )(received, jnp.asarray(device_table(devices)))


def gram_tables(devices, place, index, offset):
    square = (LANES, LANES)
    return call(
        functools.partial(gram_tables_kernel, devices),
        (struct((4, 4) + square), struct((2,) + square, jnp.int32), struct((2 * HALF, 2) + square)),
        "svv",
        flops=1 << 26,
    )(place, index, offset)


def ends(timed, gains):
    tile = struct((HALF, LANES))
    return call(ends_kernel, (tile, tile), "vv")(timed, gains)


def times_block(timed, gains):
    return call(
        times_kernel, (struct(timed.shape), struct((4, SIDE, LANES))), "vv", flops=1 << 22
    )(timed, gains)


def gram_sums(before, after, held, ids, weights):
    return call(
        gram_kernel,
        struct((2 * LANES, LANES)),
        "vvvvv",
        [pltpu.VMEM((4, SIDE + 2 * HALF, LANES), F32), pltpu.VMEM((2, LANES, LANES), F32)],
        1 << 24,
    )(before, after, held, ids, weights)


def local(samples, gram_index, gram_offset):
    inner, outer = lax.axis_size("inner"), lax.axis_size("outer")
    devices = inner * outer
    place = (lax.axis_index("inner") * outer + lax.axis_index("outer")).astype(jnp.int32)
    spot = place.reshape(1)
    points = samples.shape[2]
    parts = segment_transform(devices, spot, samples.reshape(2, points // LANES, LANES))
    received = lax.all_to_all(parts.reshape(devices, 16, LANES), AXES, 0, 0, tiled=True)
    real = device_transform(devices, received.reshape(16 * devices, LANES))
    rows = gram_index.shape[0] // LANES
    real, index, offset = lax.optimization_barrier(
        (real, gram_index.reshape(rows, LANES), gram_offset.reshape(rows, LANES))
    )
    timed = lax.all_to_all(real.reshape(devices, 8, LANES), AXES, 0, 0, tiled=True)
    gains, ids, weights = gram_tables(devices, spot, index, offset)
    timed = timed.reshape(8 * devices, LANES)
    first, last = ends(timed, gains)
    up = [(i, i + 1) for i in range(devices - 1)]
    before = lax.ppermute(last, AXES, up)
    after = lax.ppermute(first, AXES, [(j, i) for i, j in up])
    z_field, held = times_block(timed, gains)
    gram = gram_sums(before, after, held, ids, weights)
    return z_field.reshape(points), gram.reshape(-1)


def solution(mesh):
    return jax.shard_map(
        local,
        mesh=mesh,
        in_specs=(P(None, AXES, None), P(AXES), P(AXES)),
        out_specs=(P(AXES), P(AXES)),
        check_vma=False,
    )
```

```python
import functools
import math

import jax
import jax.numpy as jnp
import numpy as np
from jax import lax
from jax.experimental import pallas as pl
from jax.experimental.pallas import tpu as pltpu
from jax.sharding import PartitionSpec as P

GAP = 8
HALF = 16
UPS = 32
RATE = 4.0
SPREAD = HALF / 2.0
SIDE = 512
LANES = 128
ROWS = 9
AXES = ("inner", "outer")
F32 = jnp.float32
BF16 = jnp.bfloat16
MIB = 1 << 20


def halves(table):
    high = table.astype(jnp.bfloat16)
    low = (table - high.astype(np.float64)).astype(jnp.bfloat16)
    return np.stack([high, low])


def segment_tables():
    sample = np.arange(LANES)
    tables = []
    for g in range(4):
        angle = 2.0 * np.pi * ((4 * sample[:, None] + g) * sample[None, :] % SIDE) / SIDE
        cos, sin = np.cos(angle), np.sin(angle)
        tables.append(np.block([[cos, sin], [-sin, cos]]))
    return halves(np.stack(tables))


def twiddle_table():
    u = np.arange(SIDE).reshape(LANES, 4).T.reshape(SIDE)
    c = np.arange(SIDE)
    angle = -2.0 * np.pi * (u[:, None] * c[None, :]) / (SIDE * SIDE)
    return np.stack([np.cos(angle), np.sin(angle)]).astype(np.float32)


def device_table(devices):
    n = np.arange(devices)
    angle = 2.0 * np.pi * (n[:, None] * n[None, :] % devices) / devices
    return halves(np.concatenate([np.cos(angle), np.sin(angle)], axis=1))


def split(x):
    high = x.astype(BF16)
    return high, (x - high.astype(F32)).astype(BF16)


def dot(a, b, dims):
    return lax.dot_general(a, b, (dims, ((), ())), preferred_element_type=F32)


def dot3(a, b, dims=((1,), (0,))):
    (a_high, a_low), (b_high, b_low) = a, b
    return dot(a_high, b_high, dims) + (dot(a_high, b_low, dims) + dot(a_low, b_high, dims))


def quarter(parts):
    (r0, i0), (r1, i1), (r2, i2), (r3, i3) = parts
    ar, ai, br, bi = r0 + r2, i0 + i2, r0 - r2, i0 - i2
    cr, ci, er, ei = r1 + r3, i1 + i3, r1 - r3, i1 - i3
    return [(ar + cr, ai + ci), (br + ei, bi - er), (ar - cr, ai - ci), (br - ei, bi + er)]


def times(a, b):
    return a[0] * b[0] - a[1] * b[1], a[0] * b[1] + a[1] * b[0]


def segment_kernel(
    devices, place_ref, x_hbm, table_hbm, twiddle_hbm, out_hbm,
    x_ref, table_ref, twiddle_ref, first_ref, second_ref, out_ref, sems,
):
    place = place_ref[0]
    length = SIDE * SIDE * devices
    loads = []
    for part in range(2):
        for i in range(4):
            rows = pl.ds(SIDE * i, SIDE)
            loads.append((x_hbm.at[part, rows], x_ref.at[part, rows]))
    loads.append((table_hbm, table_ref))
    for g in range(4):
        rows = pl.ds(LANES * g, LANES)
        loads.append((twiddle_hbm.at[:, rows], twiddle_ref.at[:, rows]))
    copies = [
        pltpu.make_async_copy(source, target, sems.at[k]) for k, (source, target) in enumerate(loads)
    ]
    for copy in copies:
        copy.start()
    for copy in copies[:8]:
        copy.wait()
    for j in range(4):
        grid = [
            tuple(x_ref[part, pl.ds(SIDE * i + j, LANES, stride=4), :] for part in range(2))
            for i in range(4)
        ]
        for g, pair in enumerate(quarter(grid)):
            for part in range(2):
                high, low = split(pair[part])
                rows, cols = pl.ds(LANES * part, LANES), pl.ds(LANES * j, LANES)
                first_ref[0, g, rows, cols] = high
                first_ref[1, g, rows, cols] = low
    copies[8].wait()
    for half in range(2):
        for upper in range(2):
            g = 2 * upper + half
            done = dot3((table_ref[0, g], table_ref[1, g]), (first_ref[0, g], first_ref[1, g]))
            u = 4 * lax.broadcasted_iota(jnp.int32, (LANES, LANES), 0) + g
            angle = (place * u).astype(F32) * (-2.0 * math.pi / length)
            square = angle * angle
            turn = (
                1.0 - square * (0.5 - square * (1.0 / 24.0)),
                angle * (1.0 - square * (1.0 / 6.0 - square * (1.0 / 120.0))),
            )
            rows = pl.ds(LANES * g, LANES)
            grid = []
            copies[9 + g].wait()
            for j in range(4):
                cols = slice(LANES * j, LANES * (j + 1))
                both = times((twiddle_ref[0, rows, cols], twiddle_ref[1, rows, cols]), turn)
                grid.append(times((done[:LANES, cols], done[LANES:, cols]), both))
            for h, pair in enumerate(quarter(grid)):
                for part in range(2):
                    high, low = split(pair[part])
                    rows, cols = pl.ds(LANES * upper, LANES), pl.ds(LANES * part, LANES)
                    second_ref[0, half, h, rows, cols] = high
                    second_ref[1, half, h, rows, cols] = low
        for h in range(4):
            done = dot3(
                (second_ref[0, half, h], second_ref[1, half, h]),
                (table_ref[0, h], table_ref[1, h]),
                ((1,), (1,)),
            )
            v = 4 * lax.broadcasted_iota(jnp.int32, (8, LANES), 1) + h
            angle = (place * v).astype(F32) * (-2.0 * math.pi * SIDE / length)
            turn = (jnp.cos(angle)[:1], jnp.sin(angle)[:1])
            pair = times((done[:, :LANES], done[:, LANES:]), turn)
            for part in range(2):
                for upper in range(2):
                    start = 16 * LANES * half + 8 * part + 4 * upper + h
                    out_ref[pl.ds(start, LANES, stride=16), :] = pair[part][
                        LANES * upper : LANES * (upper + 1)
                    ]
        rows = pl.ds(16 * LANES * half, 16 * LANES)
        copy = pltpu.make_async_copy(out_ref.at[rows], out_hbm.at[rows], sems.at[13 + half])
        copy.start()
        copies.append(copy)
    for copy in copies[13:]:
        copy.wait()


def device_kernel(devices, x_ref, table_ref, out_ref):
    edges = {}
    for block in range(4):
        columns = []
        for e in (2 * block, 2 * block + 1):
            columns.append(
                jnp.concatenate(
                    [x_ref[pl.ds(8 * part + e, devices, stride=16), :] for part in range(2)], axis=0
                )
            )
        x = jnp.concatenate(columns, axis=1)
        done = dot3((table_ref[0], table_ref[1]), split(x))
        for i, e in enumerate((2 * block, 2 * block + 1)):
            values = done[:, LANES * i : LANES * (i + 1)]
            out_ref[pl.ds(e, devices, stride=ROWS), :] = values
            if e % 4 in (0, 3):
                edges[e] = values
    lane = lax.broadcasted_iota(jnp.int32, (devices, LANES), 1)
    row = lax.broadcasted_iota(jnp.int32, (devices, LANES), 0)
    after = jnp.where(lane == 0, edges[0], pltpu.roll(edges[4], 1, 1))
    before = jnp.where(lane == LANES - 1, edges[3], pltpu.roll(edges[7], LANES - 1, 1))
    after = jnp.where(row == devices - 1, 0.0, pltpu.roll(after, devices - 1, 0))
    before = jnp.where(row == 0, 0.0, pltpu.roll(before, 1, 0))
    out_ref[pl.ds(8, devices, stride=ROWS), :] = jnp.where(lane < 2, after, before)


def gain(devices, place, position):
    length = SIDE * SIDE * devices
    centred = place.astype(F32) / devices + position.astype(F32) / length - 0.5
    return length ** (-0.5) * jnp.exp(RATE * centred * centred)


def gram_tables_kernel(
    devices, place_ref, index_ref, offset_ref, gain_ref, edge_ref, ids_ref, weights_ref
):
    place = place_ref[0]
    t = lax.broadcasted_iota(jnp.int32, (LANES, LANES), 0)
    lane = lax.broadcasted_iota(jnp.int32, (LANES, LANES), 1)
    for h in range(4):
        for g in range(4):
            position = SIDE * (4 * lane + h) + 4 * t + g
            gain_ref[h, g] = gain(devices, place, position)
    u = t[:HALF]
    edge_ref[0] = gain(devices, place - 1, u + (SIDE * SIDE - HALF))
    edge_ref[1] = gain(devices, place + 1, u)
    for odd in range(2):
        ids_ref[odd] = index_ref[pl.ds(odd, LANES, stride=2), :].T
        fraction = offset_ref[pl.ds(odd, LANES, stride=2), :].T.astype(F32) * (1.0 / UPS)
        put_weights(weights_ref, odd, fraction)


def put_weights(weights_ref, odd, fraction):
    near = jnp.exp(fraction * fraction * (-0.5 / (SPREAD * SPREAD)))
    sine = jnp.sin(math.pi * fraction) * (near / math.pi)
    up = jnp.exp(fraction * (1.0 / (SPREAD * SPREAD)))
    down = jnp.exp(fraction * (-1.0 / (SPREAD * SPREAD)))
    square = fraction * fraction
    ups, downs = sine * up, sine * down
    for w in range(1, HALF + 1):
        scale = (-1.0) ** w * math.exp(-0.5 * w * w / (SPREAD * SPREAD))
        share = scale / (square - w * w)
        weights_ref[HALF - 1 + w, odd] = ups * ((fraction + w) * share)
        if w < HALF:
            weights_ref[HALF - 1 - w, odd] = downs * ((fraction - w) * share)
        ups, downs = ups * up, downs * down
    at_zero = fraction == 0.0
    weights_ref[HALF - 1, odd] = jnp.where(at_zero, 1.0, sine / jnp.where(at_zero, 1.0, fraction))


def times_kernel(x_ref, gain_ref, edge_ref, ids_ref, weights_ref, z_hbm, gram_ref, zs_ref, z_ref, ends_ref, sums, sem):
    pad = HALF
    for h in range(4):
        for g in range(4):
            start = ROWS * LANES * (g % 2) + 4 * (g // 2) + h
            raw = x_ref[pl.ds(start, LANES, stride=ROWS), :]
            zs_ref[h, pl.ds(pad + g, LANES, stride=4), :] = raw * gain_ref[h, g]
        for block in range(4):
            z_ref[pl.ds(4 * h + block, LANES, stride=16), :] = zs_ref[
                h, pl.ds(pad + LANES * block, LANES), :
            ].T
    copy = pltpu.make_async_copy(z_ref, z_hbm, sem)
    copy.start()
    for g in range(4):
        upper = g // 2
        for side, t, shift in ((0, LANES - 8, 1 + upper), (1, 0, LANES - 1 - upper)):
            start = ROWS * (LANES * (g % 2) + t) + 8
            tile = pltpu.roll(x_ref[pl.ds(start, 8, stride=ROWS), :], shift, 1)
            ends_ref[side, pl.ds(g, 8, stride=4), :] = tile
    lane = lax.broadcasted_iota(jnp.int32, (pad, LANES), 1)
    for h in range(4):
        before = zs_ref[(h - 1) % 4, pl.ds(SIDE, pad), :]
        after = zs_ref[(h + 1) % 4, pl.ds(pad, pad), :]
        if h == 0:
            edge = ends_ref[0, pl.ds(pad, pad), :] * edge_ref[0]
            before = jnp.where(lane == 0, edge, pltpu.roll(before, 1, 1))
        if h == 3:
            edge = ends_ref[1, pl.ds(0, pad), :] * edge_ref[1]
            after = jnp.where(lane == LANES - 1, edge, pltpu.roll(after, LANES - 1, 1))
        zs_ref[h, pl.ds(0, pad), :] = before
        zs_ref[h, pl.ds(pad + SIDE, pad), :] = after
    for h in range(4):

        def body(step, carry, h=h):
            rows = pl.ds(pl.multiple_of(64 * (h % 2) + 8 * step, 8), 8)
            index = ids_ref[h // 2, rows, :]
            taps = [
                zs_ref[h, pl.ds(pad + o + 64 * step, 8, stride=8), :]
                for o in range(1 - HALF, HALF + GAP)
            ]
            for bit in (2, 1, 0):
                size = 1 << bit
                chosen = (index >> bit & 1) == 1
                taps = [jnp.where(chosen, b, a) for a, b in zip(taps[:-size], taps[size:])]
            terms = [tap * weights_ref[w, h // 2, rows, :] for w, tap in enumerate(taps)]
            while len(terms) > 1:
                terms = [a + b for a, b in zip(terms[::2], terms[1::2])]
            sums[h // 2, rows, :] = terms[0]
            return carry

        lax.fori_loop(0, 8, body, 0)
    for odd in range(2):
        gram_ref[pl.ds(odd, LANES, stride=2), :] = sums[odd].T
    copy.wait()


def call(kernel, out_shape, specs, scratch=(), flops=0, limit=16, outs="v"):
    spaces = {"s": pltpu.SMEM, "v": pltpu.VMEM, "h": pltpu.HBM}
    out_specs = [pl.BlockSpec(memory_space=spaces[spec]) for spec in outs]
    if len(outs) == 1:
        out_specs = out_specs[0]
    return pl.pallas_call(
        kernel,
        out_shape=out_shape,
        in_specs=[pl.BlockSpec(memory_space=spaces[spec]) for spec in specs],
        out_specs=out_specs,
        scratch_shapes=list(scratch),
        compiler_params=pltpu.CompilerParams(vmem_limit_bytes=limit * MIB),
        cost_estimate=pl.CostEstimate(flops=flops, bytes_accessed=4 * MIB, transcendentals=0),
    )


def struct(shape, kind=F32):
    return jax.ShapeDtypeStruct(tuple(shape), kind)


def segment_transform(devices, place, samples):
    points = samples.size // 2
    table, twiddle = segment_tables(), twiddle_table()
    return call(
        functools.partial(segment_kernel, devices),
        struct((points * 2 // LANES, LANES)),
        "shhh",
        [
            pltpu.VMEM(samples.shape, F32),
            pltpu.VMEM(table.shape, BF16),
            pltpu.VMEM(twiddle.shape, F32),
            pltpu.VMEM((2, 4, 2 * LANES, SIDE), BF16),
            pltpu.VMEM((2, 2, 4, 2 * LANES, 2 * LANES), BF16),
            pltpu.VMEM((points * 2 // LANES, LANES), F32),
            pltpu.SemaphoreType.DMA((15,)),
        ],
        3 * 2 * 8 * SIDE * SIDE * LANES,
        60,
        "h",
    )(place, samples, jnp.asarray(table), jnp.asarray(twiddle))


def device_transform(devices, received):
    return call(
        functools.partial(device_kernel, devices),
        struct((ROWS * devices, LANES)),
        "vv",
        flops=3 * 2 * 2 * devices * received.shape[0] // 2 * LANES,
    )(received, jnp.asarray(device_table(devices)))


def gram_tables(devices, place, index, offset):
    square = (LANES, LANES)
    return call(
        functools.partial(gram_tables_kernel, devices),
        (
            struct((4, 4) + square),
            struct((2, HALF, LANES)),
            struct((2,) + square, jnp.int32),
            struct((2 * HALF, 2) + square),
        ),
        "svv",
        flops=1 << 26,
        outs="vvvv",
    )(place, index, offset)


def times_block(timed, tables):
    rows = SIDE * SIDE // LANES
    return call(
        times_kernel,
        (struct((rows, LANES)), struct((2 * LANES, LANES))),
        "vvvvv",
        [
            pltpu.VMEM((4, SIDE + 2 * HALF, LANES), F32),
            pltpu.VMEM((rows, LANES), F32),
            pltpu.VMEM((2, 2 * HALF, LANES), F32),
            pltpu.VMEM((2, LANES, LANES), F32),
            pltpu.SemaphoreType.DMA(()),
        ],
        1 << 24,
        outs="hv",
    )(timed, *tables)


def local(samples, gram_index, gram_offset):
    inner, outer = lax.axis_size("inner"), lax.axis_size("outer")
    devices = inner * outer
    place = (lax.axis_index("inner") * outer + lax.axis_index("outer")).astype(jnp.int32)
    spot = place.reshape(1)
    points = samples.shape[2]
    parts = segment_transform(devices, spot, samples.reshape(2, points // LANES, LANES))
    received = lax.all_to_all(parts.reshape(devices, 16, LANES), AXES, 0, 0, tiled=True)
    real = device_transform(devices, received.reshape(16 * devices, LANES))
    rows = gram_index.shape[0] // LANES
    real, index, offset = lax.optimization_barrier(
        (real, gram_index.reshape(rows, LANES), gram_offset.reshape(rows, LANES))
    )
    timed = lax.all_to_all(real.reshape(-1), AXES, 0, 0, tiled=True)
    tables = gram_tables(devices, spot, index, offset)
    z_field, gram = times_block(timed.reshape(ROWS * devices, LANES), tables)
    return z_field.reshape(points), gram.reshape(-1)


def solution(mesh):
    return jax.shard_map(
        local,
        mesh=mesh,
        in_specs=(P(None, AXES, None), P(AXES), P(AXES)),
        out_specs=(P(AXES), P(AXES)),
        check_vma=False,
    )
```

```python
import functools
import math

import jax
import jax.numpy as jnp
import numpy as np
from jax import lax
from jax.experimental import pallas as pl
from jax.experimental.pallas import tpu as pltpu
from jax.sharding import PartitionSpec as P

GAP = 8
HALF = 16
UPS = 32
RATE = 4.0
SPREAD = HALF / 2.0
SIDE = 512
LANES = 128
KEPT = 13
ROWS = 9
AXES = ("inner", "outer")
F32 = jnp.float32
BF16 = jnp.bfloat16
MIB = 1 << 20


def halves(table):
    high = table.astype(jnp.bfloat16)
    low = (table - high.astype(np.float64)).astype(jnp.bfloat16)
    return np.stack([high, low])


def device_table(devices):
    n = np.arange(devices)
    angle = 2.0 * np.pi * (n[:, None] * n[None, :] % devices) / devices
    return halves(np.concatenate([np.cos(angle), np.sin(angle)], axis=1))


def split(x):
    high = x.astype(BF16)
    return high, (x - high.astype(F32)).astype(BF16)


def dot(a, b, dims):
    return lax.dot_general(a, b, (dims, ((), ())), preferred_element_type=F32)


def dot3(a, b, dims=((1,), (0,))):
    (a_high, a_low), (b_high, b_low) = a, b
    return dot(a_high, b_high, dims) + (dot(a_high, b_low, dims) + dot(a_low, b_high, dims))


def quarter(parts):
    (r0, i0), (r1, i1), (r2, i2), (r3, i3) = parts
    ar, ai, br, bi = r0 + r2, i0 + i2, r0 - r2, i0 - i2
    cr, ci, er, ei = r1 + r3, i1 + i3, r1 - r3, i1 - i3
    return [(ar + cr, ai + ci), (br + ei, bi - er), (ar - cr, ai - ci), (br - ei, bi + er)]


def times(a, b):
    return a[0] * b[0] - a[1] * b[1], a[0] * b[1] + a[1] * b[0]


def unit(count, period):
    half = period // 2
    near = ((count + half) & (period - 1)) - half
    angle = near.astype(F32) * (0.5 * math.pi / period)
    square = angle * angle
    sine, cosine = 1.0, 1.0
    for n in (4, 3, 2, 1):
        sine = 1.0 - square * (1.0 / ((2 * n) * (2 * n + 1))) * sine
    for n in (5, 4, 3, 2, 1):
        cosine = 1.0 - square * (1.0 / ((2 * n - 1) * (2 * n))) * cosine
    sine = angle * sine
    for _ in range(2):
        sine, cosine = 2.0 * sine * cosine, 1.0 - 2.0 * sine * sine
    return cosine, -sine


def segment_kernel(devices, place_ref, x_ref, out_ref, table_ref, first_ref, second_ref):
    place = place_ref[0]
    points = SIDE * SIDE
    row = lax.broadcasted_iota(jnp.int32, (LANES, LANES), 0)
    lane = lax.broadcasted_iota(jnp.int32, (LANES, LANES), 1)
    line = lax.broadcasted_iota(jnp.int32, (8, LANES), 1)
    whole = unit(row * lane, LANES)
    for g in range(4):
        here = whole
        if g:
            here = times(whole, tuple(x[:1] for x in unit(line * g, SIDE)))
        (cos_high, cos_low), (sin_high, sin_low) = split(here[0]), split(-here[1])
        for k, (cos, sin) in enumerate(((cos_high, sin_high), (cos_low, sin_low))):
            table_ref[k, g, :LANES, :LANES] = cos
            table_ref[k, g, :LANES, LANES:] = sin
            table_ref[k, g, LANES:, :LANES] = -sin
            table_ref[k, g, LANES:, LANES:] = cos
    for j in range(4):
        grid = [
            tuple(x_ref[part, pl.ds(SIDE * i + j, LANES, stride=4), :] for part in range(2))
            for i in range(4)
        ]
        for g, pair in enumerate(quarter(grid)):
            for part in range(2):
                high, low = split(pair[part])
                rows, cols = pl.ds(LANES * part, LANES), pl.ds(LANES * j, LANES)
                first_ref[0, g, rows, cols] = high
                first_ref[1, g, rows, cols] = low
    across = unit(row * lane, points // 4)
    down = unit(row, SIDE)
    for g in range(4):
        done = dot3((table_ref[0, g], table_ref[1, g]), (first_ref[0, g], first_ref[1, g]))
        both = times(across, unit(place * (4 * row + g), points * devices))
        step = down
        if g:
            both = times(both, tuple(x[:1] for x in unit(line * g, points)))
            angle = -2.0 * math.pi * g * LANES / points
            step = times(down, (math.cos(angle), math.sin(angle)))
        grid = []
        for j in range(4):
            cols = slice(LANES * j, LANES * (j + 1))
            if j:
                both = times(both, step)
            grid.append(times((done[:LANES, cols], done[LANES:, cols]), both))
        for h, pair in enumerate(quarter(grid)):
            for part in range(2):
                high, low = split(pair[part])
                rows, cols = pl.ds(LANES * g, LANES), pl.ds(LANES * part, LANES)
                second_ref[0, h, rows, cols] = high
                second_ref[1, h, rows, cols] = low
    for h in range(4):
        done = dot3(
            (second_ref[0, h], second_ref[1, h]), (table_ref[0, h], table_ref[1, h]), ((1,), (1,))
        )
        turn = tuple(x[:1] for x in unit(place * (4 * line + h), SIDE * devices))
        pair = times((done[:, :LANES], done[:, LANES:]), turn)
        for part in range(2):
            for upper in range(2):
                out_ref[pl.ds(8 * part + 4 * upper + h, SIDE // 2, stride=16), :] = pair[part][
                    SIDE // 2 * upper : SIDE // 2 * (upper + 1)
                ]


def device_kernel(devices, x_ref, table_ref, out_ref):
    edges = {}
    for block in range(4):
        columns = []
        for e in (2 * block, 2 * block + 1):
            columns.append(
                jnp.concatenate(
                    [x_ref[pl.ds(8 * part + e, devices, stride=16), :] for part in range(2)], axis=0
                )
            )
        x = jnp.concatenate(columns, axis=1)
        done = dot3((table_ref[0], table_ref[1]), split(x))
        for i, e in enumerate((2 * block, 2 * block + 1)):
            values = done[:, LANES * i : LANES * (i + 1)]
            out_ref[pl.ds(e, devices, stride=ROWS), :] = values
            if e % 4 in (0, 3):
                edges[e] = values
    lane = lax.broadcasted_iota(jnp.int32, (devices, LANES), 1)
    row = lax.broadcasted_iota(jnp.int32, (devices, LANES), 0)
    after = jnp.where(lane == 0, edges[0], pltpu.roll(edges[4], 1, 1))
    before = jnp.where(lane == LANES - 1, edges[3], pltpu.roll(edges[7], LANES - 1, 1))
    after = jnp.where(row == devices - 1, 0.0, pltpu.roll(after, devices - 1, 0))
    before = jnp.where(row == 0, 0.0, pltpu.roll(before, 1, 0))
    out_ref[pl.ds(8, devices, stride=ROWS), :] = jnp.where(lane < 2, after, before)


def gain(devices, place, position):
    length = SIDE * SIDE * devices
    centred = place.astype(F32) / devices + position.astype(F32) / length - 0.5
    return length ** (-0.5) * jnp.exp(RATE * centred * centred)


def gram_tables_kernel(index_ref, offset_ref, code_ref, share_ref, entry_ref):
    for odd in range(2):
        rows = pl.ds(odd, LANES, stride=2)
        code = (offset_ref[rows, :] * GAP + index_ref[rows, :]).T
        code_ref[odd] = code
        fraction = (code >> 3).astype(F32) * (1.0 / UPS)
        for w, share in enumerate(shares_of(fraction)[:KEPT]):
            share_ref[w, odd] = share
    line = lax.broadcasted_iota(jnp.int32, (8, LANES), 1) & (UPS - 1)
    for w, share in enumerate(shares_of(line.astype(F32) * (1.0 / UPS))[KEPT:]):
        entry_ref[w] = share


def shares_of(fraction):
    sine = jnp.sin(math.pi * fraction) * (1.0 / math.pi)
    sine = sine * jnp.exp(fraction * fraction * (-0.5 / (SPREAD * SPREAD)))
    at_zero = fraction == 0.0
    shares = [jnp.where(at_zero, 1.0, sine / jnp.where(at_zero, 1.0, fraction))]
    square = fraction * fraction
    for w in range(1, HALF + 1):
        scale = (-1.0) ** w * math.exp(-0.5 * w * w / (SPREAD * SPREAD))
        shares.append(sine * (scale / (square - w * w)))
    shares.append(jnp.exp(fraction * (1.0 / (SPREAD * SPREAD))))
    shares.append(jnp.exp(fraction * (-1.0 / (SPREAD * SPREAD))))
    return shares


def weighted(taps, shares, fraction):
    up, down = shares[HALF + 1], shares[HALF + 2]
    ups, downs = up, down
    terms = [taps[HALF - 1] * shares[0]]
    for w in range(1, HALF + 1):
        term = (ups * taps[HALF - 1 + w]) * (fraction + w)
        if w < HALF:
            term = term + (downs * taps[HALF - 1 - w]) * (fraction - w)
        terms.append(term * shares[w])
        ups, downs = ups * up, downs * down
    while len(terms) > 1:
        terms = [a + b for a, b in zip(terms[::2], terms[1::2])] + terms[len(terms) & ~1 :]
    return terms[0]


def times_kernel(
    devices, place_ref, x_ref, code_ref, share_ref, entry_ref, z_hbm, gram_ref,
    zs_ref, z_ref, ends_ref, sums, sem,
):
    pad = HALF
    place = place_ref[0]
    length = SIDE * SIDE * devices
    t = lax.broadcasted_iota(jnp.int32, (LANES, LANES), 0)
    line = lax.broadcasted_iota(jnp.int32, (8, LANES), 1)
    for h in range(4):
        begin = SIDE * (4 * line + h)
        base = gain(devices, place, begin)[:1]
        start_c = (place.astype(F32) / devices + begin.astype(F32) / length - 0.5)[:1]
        for g in range(4):
            start = ROWS * LANES * (g % 2) + 4 * (g // 2) + h
            raw = x_ref[pl.ds(start, LANES, stride=ROWS), :]
            du = (4 * t + g).astype(F32) * (1.0 / length)
            x = (du * (2.0 * RATE)) * (start_c + 0.5 * du)
            factor = base + base * (x + 0.5 * x * x)
            zs_ref[h, pl.ds(pad + g, LANES, stride=4), :] = raw * factor
        for block in range(4):
            z_ref[pl.ds(4 * h + block, LANES, stride=16), :] = zs_ref[
                h, pl.ds(pad + LANES * block, LANES), :
            ].T
    copy = pltpu.make_async_copy(z_ref, z_hbm, sem)
    copy.start()
    for g in range(4):
        upper = g // 2
        for side, top, shift in ((0, LANES - 8, 1 + upper), (1, 0, LANES - 1 - upper)):
            start = ROWS * (LANES * (g % 2) + top) + 8
            tile = pltpu.roll(x_ref[pl.ds(start, 8, stride=ROWS), :], shift, 1)
            ends_ref[side, pl.ds(g, 8, stride=4), :] = tile
    lane = lax.broadcasted_iota(jnp.int32, (pad, LANES), 1)
    for h in range(4):
        before = zs_ref[(h - 1) % 4, pl.ds(SIDE, pad), :]
        after = zs_ref[(h + 1) % 4, pl.ds(pad, pad), :]
        if h == 0:
            edge = ends_ref[0, pl.ds(pad, pad), :] * gain(
                devices, place - 1, t[:pad] + (SIDE * SIDE - HALF)
            )
            before = jnp.where(lane == 0, edge, pltpu.roll(before, 1, 1))
        if h == 3:
            edge = ends_ref[1, pl.ds(0, pad), :] * gain(devices, place + 1, t[:pad])
            after = jnp.where(lane == LANES - 1, edge, pltpu.roll(after, LANES - 1, 1))
        zs_ref[h, pl.ds(0, pad), :] = before
        zs_ref[h, pl.ds(pad + SIDE, pad), :] = after
    for h in range(4):

        def body(step, carry, h=h):
            rows = pl.ds(pl.multiple_of(64 * (h % 2) + 8 * step, 8), 8)
            index = code_ref[h // 2, rows, :]
            offset = index >> 3
            fraction = offset.astype(F32) * (1.0 / UPS)
            taps = [
                zs_ref[h, pl.ds(pad + o + 64 * step, 8, stride=8), :]
                for o in range(1 - HALF, HALF + GAP)
            ]
            for bit in (2, 1, 0):
                size = 1 << bit
                chosen = (index >> bit & 1) == 1
                taps = [jnp.where(chosen, b, a) for a, b in zip(taps[:-size], taps[size:])]
            shares = [share_ref[w, h // 2, rows, :] for w in range(KEPT)]
            for w in range(HALF + 3 - KEPT):
                shares.append(jnp.take_along_axis(entry_ref[w], offset, axis=1))
            sums[h // 2, rows, :] = weighted(taps, shares, fraction)
            return carry

        lax.fori_loop(0, 8, body, 0, unroll=4)
    for odd in range(2):
        gram_ref[pl.ds(odd, LANES, stride=2), :] = sums[odd].T
    copy.wait()


def call(kernel, out_shape, specs, scratch=(), flops=0, limit=16, outs="v"):
    spaces = {"s": pltpu.SMEM, "v": pltpu.VMEM, "h": pltpu.HBM}
    out_specs = [pl.BlockSpec(memory_space=spaces[spec]) for spec in outs]
    if len(outs) == 1:
        out_specs = out_specs[0]
    return pl.pallas_call(
        kernel,
        out_shape=out_shape,
        in_specs=[pl.BlockSpec(memory_space=spaces[spec]) for spec in specs],
        out_specs=out_specs,
        scratch_shapes=list(scratch),
        compiler_params=pltpu.CompilerParams(vmem_limit_bytes=limit * MIB),
        cost_estimate=pl.CostEstimate(flops=flops, bytes_accessed=4 * MIB, transcendentals=0),
    )


def struct(shape, kind=F32):
    return jax.ShapeDtypeStruct(tuple(shape), kind)


def segment_transform(devices, place, samples):
    points = samples.size // 2
    return call(
        functools.partial(segment_kernel, devices),
        struct((points * 2 // LANES, LANES)),
        "sv",
        [
            pltpu.VMEM((2, 4, 2 * LANES, 2 * LANES), BF16),
            pltpu.VMEM((2, 4, 2 * LANES, SIDE), BF16),
            pltpu.VMEM((2, 4, SIDE, 2 * LANES), BF16),
        ],
        3 * 2 * 8 * SIDE * SIDE * LANES,
    )(place, samples)


def device_transform(devices, received):
    return call(
        functools.partial(device_kernel, devices),
        struct((ROWS * devices, LANES)),
        "vv",
        flops=3 * 2 * 2 * devices * received.shape[0] // 2 * LANES,
    )(received, jnp.asarray(device_table(devices)))


def gram_tables(index, offset):
    square = (2, LANES, LANES)
    return call(
        gram_tables_kernel,
        (
            struct(square, jnp.int32),
            struct((KEPT,) + square),
            struct((HALF + 3 - KEPT, 8, LANES)),
        ),
        "vv",
        flops=1 << 26,
        outs="vvv",
    )(index, offset)


def times_block(devices, place, timed, tables):
    rows = SIDE * SIDE // LANES
    return call(
        functools.partial(times_kernel, devices),
        (struct((rows, LANES)), struct((2 * LANES, LANES))),
        "svvvv",
        [
            pltpu.VMEM((4, SIDE + 2 * HALF, LANES), F32),
            pltpu.VMEM((rows, LANES), F32),
            pltpu.VMEM((2, 2 * HALF, LANES), F32),
            pltpu.VMEM((2, LANES, LANES), F32),
            pltpu.SemaphoreType.DMA(()),
        ],
        1 << 24,
        outs="hv",
    )(place, timed, *tables)


def local(samples, gram_index, gram_offset):
    inner, outer = lax.axis_size("inner"), lax.axis_size("outer")
    devices = inner * outer
    place = (lax.axis_index("inner") * outer + lax.axis_index("outer")).astype(jnp.int32)
    spot = place.reshape(1)
    points = samples.shape[2]
    parts = segment_transform(devices, spot, samples.reshape(2, points // LANES, LANES))
    received = lax.all_to_all(parts.reshape(devices, 16, LANES), AXES, 0, 0, tiled=True)
    real = device_transform(devices, received.reshape(16 * devices, LANES))
    rows = gram_index.shape[0] // LANES
    real, index, offset = lax.optimization_barrier(
        (real, gram_index.reshape(rows, LANES), gram_offset.reshape(rows, LANES))
    )
    timed = lax.all_to_all(real.reshape(-1), AXES, 0, 0, tiled=True)
    tables = gram_tables(index, offset)
    z_field, gram = times_block(
        devices, spot, timed.reshape(ROWS * devices, LANES), tables
    )
    return z_field.reshape(points), gram.reshape(-1)


def solution(mesh):
    return jax.shard_map(
        local,
        mesh=mesh,
        in_specs=(P(None, AXES, None), P(AXES), P(AXES)),
        out_specs=(P(AXES), P(AXES)),
        check_vma=False,
    )
```

```python
import functools
import math

import jax
import jax.numpy as jnp
import numpy as np
from jax import lax
from jax.experimental import pallas as pl
from jax.experimental.pallas import tpu as pltpu
from jax.sharding import PartitionSpec as P

GAP = 8
HALF = 16
UPS = 32
RATE = 4.0
SPREAD = HALF / 2.0
SIDE = 512
LANES = 128
KEPT = 13
ROWS = 9
AXES = ("inner", "outer")
F32 = jnp.float32
BF16 = jnp.bfloat16
MIB = 1 << 20


def halves(table):
    high = table.astype(jnp.bfloat16)
    low = (table - high.astype(np.float64)).astype(jnp.bfloat16)
    return np.stack([high, low])


def device_table(devices):
    n = np.arange(devices)
    angle = 2.0 * np.pi * (n[:, None] * n[None, :] % devices) / devices
    return halves(np.concatenate([np.cos(angle), np.sin(angle)], axis=1))


def split(x):
    high = x.astype(BF16)
    return high, (x - high.astype(F32)).astype(BF16)


def dot(a, b, dims):
    return lax.dot_general(a, b, (dims, ((), ())), preferred_element_type=F32)


def dot3(a, b, dims=((1,), (0,))):
    (a_high, a_low), (b_high, b_low) = a, b
    return dot(a_high, b_high, dims) + (dot(a_high, b_low, dims) + dot(a_low, b_high, dims))


def quarter(parts):
    (r0, i0), (r1, i1), (r2, i2), (r3, i3) = parts
    ar, ai, br, bi = r0 + r2, i0 + i2, r0 - r2, i0 - i2
    cr, ci, er, ei = r1 + r3, i1 + i3, r1 - r3, i1 - i3
    return [(ar + cr, ai + ci), (br + ei, bi - er), (ar - cr, ai - ci), (br - ei, bi + er)]


def times(a, b):
    return a[0] * b[0] - a[1] * b[1], a[0] * b[1] + a[1] * b[0]


def unit(count, period):
    half = period // 2
    near = ((count + half) & (period - 1)) - half
    angle = near.astype(F32) * (0.5 * math.pi / period)
    square = angle * angle
    sine, cosine = 1.0, 1.0
    for n in (4, 3, 2, 1):
        sine = 1.0 - square * (1.0 / ((2 * n) * (2 * n + 1))) * sine
    for n in (5, 4, 3, 2, 1):
        cosine = 1.0 - square * (1.0 / ((2 * n - 1) * (2 * n))) * cosine
    sine = angle * sine
    for _ in range(2):
        sine, cosine = 2.0 * sine * cosine, 1.0 - 2.0 * sine * sine
    return cosine, -sine


def segment_tables_kernel(devices, place_ref, table_ref, twiddle_ref, turn_ref):
    place = place_ref[0]
    points = SIDE * SIDE
    row = lax.broadcasted_iota(jnp.int32, (LANES, LANES), 0)
    lane = lax.broadcasted_iota(jnp.int32, (LANES, LANES), 1)
    line = lax.broadcasted_iota(jnp.int32, (8, LANES), 1)
    whole = unit(row * lane, LANES)
    across = unit(row * lane, points // 4)
    down = unit(row, SIDE)
    for g in range(4):
        here = whole
        if g:
            here = times(whole, tuple(x[:1] for x in unit(line * g, SIDE)))
        (cos_high, cos_low), (sin_high, sin_low) = split(here[0]), split(-here[1])
        for k, (cos, sin) in enumerate(((cos_high, sin_high), (cos_low, sin_low))):
            table_ref[k, g, :LANES, :LANES] = cos
            table_ref[k, g, :LANES, LANES:] = sin
            table_ref[k, g, LANES:, :LANES] = -sin
            table_ref[k, g, LANES:, LANES:] = cos
        both = times(across, unit(place * (4 * row + g), points * devices))
        step = down
        if g:
            both = times(both, tuple(x[:1] for x in unit(line * g, points)))
            angle = -2.0 * math.pi * g * LANES / points
            step = times(down, (math.cos(angle), math.sin(angle)))
        for j in range(4):
            if j:
                both = times(both, step)
            for part in range(2):
                twiddle_ref[part, g, j] = both[part]
        turn = unit(place * (4 * line + g), SIDE * devices)
        for part in range(2):
            turn_ref[part, g] = turn[part]


def segment_kernel(x_ref, table_ref, twiddle_ref, turn_ref, out_ref, first_ref, second_ref):
    for j in range(4):
        grid = [
            tuple(x_ref[part, pl.ds(SIDE * i + j, LANES, stride=4), :] for part in range(2))
            for i in range(4)
        ]
        for g, pair in enumerate(quarter(grid)):
            for part in range(2):
                high, low = split(pair[part])
                rows, cols = pl.ds(LANES * part, LANES), pl.ds(LANES * j, LANES)
                first_ref[0, g, rows, cols] = high
                first_ref[1, g, rows, cols] = low
    for g in range(4):
        done = dot3((table_ref[0, g], table_ref[1, g]), (first_ref[0, g], first_ref[1, g]))
        grid = []
        for j in range(4):
            cols = slice(LANES * j, LANES * (j + 1))
            both = (twiddle_ref[0, g, j], twiddle_ref[1, g, j])
            grid.append(times((done[:LANES, cols], done[LANES:, cols]), both))
        for h, pair in enumerate(quarter(grid)):
            for part in range(2):
                high, low = split(pair[part])
                rows, cols = pl.ds(LANES * g, LANES), pl.ds(LANES * part, LANES)
                second_ref[0, h, rows, cols] = high
                second_ref[1, h, rows, cols] = low
    for h in range(4):
        done = dot3(
            (second_ref[0, h], second_ref[1, h]), (table_ref[0, h], table_ref[1, h]), ((1,), (1,))
        )
        pair = times((done[:, :LANES], done[:, LANES:]), (turn_ref[0, h, :1], turn_ref[1, h, :1]))
        for part in range(2):
            for upper in range(2):
                out_ref[pl.ds(8 * part + 4 * upper + h, SIDE // 2, stride=16), :] = pair[part][
                    SIDE // 2 * upper : SIDE // 2 * (upper + 1)
                ]


def device_kernel(devices, x_ref, table_ref, out_ref):
    edges = {}
    for block in range(4):
        columns = []
        for e in (2 * block, 2 * block + 1):
            columns.append(
                jnp.concatenate(
                    [x_ref[pl.ds(8 * part + e, devices, stride=16), :] for part in range(2)], axis=0
                )
            )
        x = jnp.concatenate(columns, axis=1)
        done = dot3((table_ref[0], table_ref[1]), split(x))
        for i, e in enumerate((2 * block, 2 * block + 1)):
            values = done[:, LANES * i : LANES * (i + 1)]
            out_ref[pl.ds(e, devices, stride=ROWS), :] = values
            if e % 4 in (0, 3):
                edges[e] = values
    lane = lax.broadcasted_iota(jnp.int32, (devices, LANES), 1)
    row = lax.broadcasted_iota(jnp.int32, (devices, LANES), 0)
    after = jnp.where(lane == 0, edges[0], pltpu.roll(edges[4], 1, 1))
    before = jnp.where(lane == LANES - 1, edges[3], pltpu.roll(edges[7], LANES - 1, 1))
    after = jnp.where(row == devices - 1, 0.0, pltpu.roll(after, devices - 1, 0))
    before = jnp.where(row == 0, 0.0, pltpu.roll(before, 1, 0))
    out_ref[pl.ds(8, devices, stride=ROWS), :] = jnp.where(lane < 2, after, before)


def gain(devices, place, position):
    length = SIDE * SIDE * devices
    centred = place.astype(F32) / devices + position.astype(F32) / length - 0.5
    return length ** (-0.5) * jnp.exp(RATE * centred * centred)


def gram_tables_kernel(index_ref, offset_ref, code_ref, share_ref, entry_ref):
    for odd in range(2):
        rows = pl.ds(odd, LANES, stride=2)
        code = (offset_ref[rows, :] * GAP + index_ref[rows, :]).T
        code_ref[odd] = code
        fraction = (code >> 3).astype(F32) * (1.0 / UPS)
        for w, share in enumerate(shares_of(fraction)[:KEPT]):
            share_ref[w, odd] = share
    line = lax.broadcasted_iota(jnp.int32, (8, LANES), 1) & (UPS - 1)
    for w, share in enumerate(shares_of(line.astype(F32) * (1.0 / UPS))[KEPT:]):
        entry_ref[w] = share


def shares_of(fraction):
    sine = jnp.sin(math.pi * fraction) * (1.0 / math.pi)
    sine = sine * jnp.exp(fraction * fraction * (-0.5 / (SPREAD * SPREAD)))
    at_zero = fraction == 0.0
    shares = [jnp.where(at_zero, 1.0, sine / jnp.where(at_zero, 1.0, fraction))]
    square = fraction * fraction
    for w in range(1, HALF + 1):
        scale = (-1.0) ** w * math.exp(-0.5 * w * w / (SPREAD * SPREAD))
        shares.append(sine * (scale / (square - w * w)))
    shares.append(jnp.exp(fraction * (1.0 / (SPREAD * SPREAD))))
    shares.append(jnp.exp(fraction * (-1.0 / (SPREAD * SPREAD))))
    return shares


def weighted(taps, shares, fraction):
    up, down = shares[HALF + 1], shares[HALF + 2]
    ups, downs = up, down
    terms = [taps[HALF - 1] * shares[0]]
    for w in range(1, HALF + 1):
        term = (ups * taps[HALF - 1 + w]) * (fraction + w)
        if w < HALF:
            term = term + (downs * taps[HALF - 1 - w]) * (fraction - w)
        terms.append(term * shares[w])
        ups, downs = ups * up, downs * down
    while len(terms) > 1:
        terms = [a + b for a, b in zip(terms[::2], terms[1::2])] + terms[len(terms) & ~1 :]
    return terms[0]


def times_kernel(
    devices, place_ref, x_ref, code_ref, share_ref, entry_ref, z_hbm, gram_ref,
    zs_ref, z_ref, ends_ref, sums, sem,
):
    pad = HALF
    place = place_ref[0]
    length = SIDE * SIDE * devices
    t = lax.broadcasted_iota(jnp.int32, (LANES, LANES), 0)
    line = lax.broadcasted_iota(jnp.int32, (8, LANES), 1)
    for h in range(4):
        begin = SIDE * (4 * line + h)
        base = gain(devices, place, begin)[:1]
        start_c = (place.astype(F32) / devices + begin.astype(F32) / length - 0.5)[:1]
        for g in range(4):
            start = ROWS * LANES * (g % 2) + 4 * (g // 2) + h
            raw = x_ref[pl.ds(start, LANES, stride=ROWS), :]
            du = (4 * t + g).astype(F32) * (1.0 / length)
            x = (du * (2.0 * RATE)) * (start_c + 0.5 * du)
            factor = base + base * (x + 0.5 * x * x)
            zs_ref[h, pl.ds(pad + g, LANES, stride=4), :] = raw * factor
        for block in range(4):
            z_ref[pl.ds(4 * h + block, LANES, stride=16), :] = zs_ref[
                h, pl.ds(pad + LANES * block, LANES), :
            ].T
    copy = pltpu.make_async_copy(z_ref, z_hbm, sem)
    copy.start()
    for g in range(4):
        upper = g // 2
        for side, top, shift in ((0, LANES - 8, 1 + upper), (1, 0, LANES - 1 - upper)):
            start = ROWS * (LANES * (g % 2) + top) + 8
            tile = pltpu.roll(x_ref[pl.ds(start, 8, stride=ROWS), :], shift, 1)
            ends_ref[side, pl.ds(g, 8, stride=4), :] = tile
    lane = lax.broadcasted_iota(jnp.int32, (pad, LANES), 1)
    for h in range(4):
        before = zs_ref[(h - 1) % 4, pl.ds(SIDE, pad), :]
        after = zs_ref[(h + 1) % 4, pl.ds(pad, pad), :]
        if h == 0:
            edge = ends_ref[0, pl.ds(pad, pad), :] * gain(
                devices, place - 1, t[:pad] + (SIDE * SIDE - HALF)
            )
            before = jnp.where(lane == 0, edge, pltpu.roll(before, 1, 1))
        if h == 3:
            edge = ends_ref[1, pl.ds(0, pad), :] * gain(devices, place + 1, t[:pad])
            after = jnp.where(lane == LANES - 1, edge, pltpu.roll(after, LANES - 1, 1))
        zs_ref[h, pl.ds(0, pad), :] = before
        zs_ref[h, pl.ds(pad + SIDE, pad), :] = after
    for h in range(4):

        def body(step, carry, h=h):
            rows = pl.ds(pl.multiple_of(64 * (h % 2) + 8 * step, 8), 8)
            index = code_ref[h // 2, rows, :]
            offset = index >> 3
            fraction = offset.astype(F32) * (1.0 / UPS)
            taps = [
                zs_ref[h, pl.ds(pad + o + 64 * step, 8, stride=8), :]
                for o in range(1 - HALF, HALF + GAP)
            ]
            for bit in (2, 1, 0):
                size = 1 << bit
                chosen = (index >> bit & 1) == 1
                taps = [jnp.where(chosen, b, a) for a, b in zip(taps[:-size], taps[size:])]
            shares = [share_ref[w, h // 2, rows, :] for w in range(KEPT)]
            for w in range(HALF + 3 - KEPT):
                shares.append(jnp.take_along_axis(entry_ref[w], offset, axis=1))
            sums[h // 2, rows, :] = weighted(taps, shares, fraction)
            return carry

        lax.fori_loop(0, 8, body, 0, unroll=4)
    for odd in range(2):
        gram_ref[pl.ds(odd, LANES, stride=2), :] = sums[odd].T
    copy.wait()


def call(kernel, out_shape, specs, scratch=(), flops=0, limit=16, outs="v"):
    spaces = {"s": pltpu.SMEM, "v": pltpu.VMEM, "h": pltpu.HBM}
    out_specs = [pl.BlockSpec(memory_space=spaces[spec]) for spec in outs]
    if len(outs) == 1:
        out_specs = out_specs[0]
    return pl.pallas_call(
        kernel,
        out_shape=out_shape,
        in_specs=[pl.BlockSpec(memory_space=spaces[spec]) for spec in specs],
        out_specs=out_specs,
        scratch_shapes=list(scratch),
        compiler_params=pltpu.CompilerParams(vmem_limit_bytes=limit * MIB),
        cost_estimate=pl.CostEstimate(flops=flops, bytes_accessed=4 * MIB, transcendentals=0),
    )


def struct(shape, kind=F32):
    return jax.ShapeDtypeStruct(tuple(shape), kind)


def segment_tables(devices, place):
    return call(
        functools.partial(segment_tables_kernel, devices),
        (
            struct((2, 4, 2 * LANES, 2 * LANES), BF16),
            struct((2, 4, 4, LANES, LANES)),
            struct((2, 4, 8, LANES)),
        ),
        "s",
        flops=1 << 32,
        outs="vvv",
    )(place)


def segment_transform(samples, tables):
    points = samples.size // 2
    return call(
        segment_kernel,
        struct((points * 2 // LANES, LANES)),
        "vvvv",
        [
            pltpu.VMEM((2, 4, 2 * LANES, SIDE), BF16),
            pltpu.VMEM((2, 4, SIDE, 2 * LANES), BF16),
        ],
        3 * 2 * 8 * SIDE * SIDE * LANES,
    )(samples, *tables)


def device_transform(devices, received):
    return call(
        functools.partial(device_kernel, devices),
        struct((ROWS * devices, LANES)),
        "vv",
        flops=3 * 2 * 2 * devices * received.shape[0] // 2 * LANES,
    )(received, jnp.asarray(device_table(devices)))


def gram_tables(index, offset):
    square = (2, LANES, LANES)
    return call(
        gram_tables_kernel,
        (
            struct(square, jnp.int32),
            struct((KEPT,) + square),
            struct((HALF + 3 - KEPT, 8, LANES)),
        ),
        "vv",
        flops=1 << 26,
        outs="vvv",
    )(index, offset)


def times_block(devices, place, timed, tables):
    rows = SIDE * SIDE // LANES
    return call(
        functools.partial(times_kernel, devices),
        (struct((rows, LANES)), struct((2 * LANES, LANES))),
        "svvvv",
        [
            pltpu.VMEM((4, SIDE + 2 * HALF, LANES), F32),
            pltpu.VMEM((rows, LANES), F32),
            pltpu.VMEM((2, 2 * HALF, LANES), F32),
            pltpu.VMEM((2, LANES, LANES), F32),
            pltpu.SemaphoreType.DMA(()),
        ],
        1 << 24,
        outs="hv",
    )(place, timed, *tables)


def local(samples, gram_index, gram_offset):
    inner, outer = lax.axis_size("inner"), lax.axis_size("outer")
    devices = inner * outer
    place = (lax.axis_index("inner") * outer + lax.axis_index("outer")).astype(jnp.int32)
    spot = place.reshape(1)
    points = samples.shape[2]
    rows = gram_index.shape[0] // LANES
    tables = segment_tables(devices, spot)
    tables, index, offset = lax.optimization_barrier(
        (tables, gram_index.reshape(rows, LANES), gram_offset.reshape(rows, LANES))
    )
    weights = gram_tables(index, offset)
    tables, weights = lax.optimization_barrier((tables, weights))
    parts = segment_transform(samples.reshape(2, points // LANES, LANES), tables)
    received = lax.all_to_all(parts.reshape(devices, 16, LANES), AXES, 0, 0, tiled=True)
    real = device_transform(devices, received.reshape(16 * devices, LANES))
    timed = lax.all_to_all(real.reshape(-1), AXES, 0, 0, tiled=True)
    z_field, gram = times_block(
        devices, spot, timed.reshape(ROWS * devices, LANES), weights
    )
    return z_field.reshape(points), gram.reshape(-1)


def solution(mesh):
    return jax.shard_map(
        local,
        mesh=mesh,
        in_specs=(P(None, AXES, None), P(AXES), P(AXES)),
        out_specs=(P(AXES), P(AXES)),
        check_vma=False,
    )
```

```python
import functools
import math

import jax
import jax.numpy as jnp
import numpy as np
from jax import lax
from jax.experimental import pallas as pl
from jax.experimental.pallas import tpu as pltpu
from jax.sharding import PartitionSpec as P

GAP = 8
HALF = 16
UPS = 32
RATE = 4.0
SPREAD = HALF / 2.0
SIDE = 512
LANES = 128
KEPT = 13
ROWS = 9
AXES = ("inner", "outer")
F32 = jnp.float32
BF16 = jnp.bfloat16
MIB = 1 << 20


def halves(table):
    high = table.astype(jnp.bfloat16)
    low = (table - high.astype(np.float64)).astype(jnp.bfloat16)
    return np.stack([high, low])


def device_table(devices):
    n = np.arange(devices)
    angle = 2.0 * np.pi * (n[:, None] * n[None, :] % devices) / devices
    return halves(np.concatenate([np.cos(angle), np.sin(angle)], axis=1))


def split(x):
    high = x.astype(BF16)
    return high, (x - high.astype(F32)).astype(BF16)


def dot(a, b, dims):
    return lax.dot_general(a, b, (dims, ((), ())), preferred_element_type=F32)


def dot3(a, b, dims=((1,), (0,))):
    (a_high, a_low), (b_high, b_low) = a, b
    return dot(a_high, b_high, dims) + (dot(a_high, b_low, dims) + dot(a_low, b_high, dims))


def quarter(parts):
    (r0, i0), (r1, i1), (r2, i2), (r3, i3) = parts
    ar, ai, br, bi = r0 + r2, i0 + i2, r0 - r2, i0 - i2
    cr, ci, er, ei = r1 + r3, i1 + i3, r1 - r3, i1 - i3
    return [(ar + cr, ai + ci), (br + ei, bi - er), (ar - cr, ai - ci), (br - ei, bi + er)]


def times(a, b):
    return a[0] * b[0] - a[1] * b[1], a[0] * b[1] + a[1] * b[0]


def unit(count, period):
    half = period // 2
    near = ((count + half) & (period - 1)) - half
    angle = near.astype(F32) * (0.5 * math.pi / period)
    square = angle * angle
    sine, cosine = 1.0, 1.0
    for n in (4, 3, 2, 1):
        sine = 1.0 - square * (1.0 / ((2 * n) * (2 * n + 1))) * sine
    for n in (5, 4, 3, 2, 1):
        cosine = 1.0 - square * (1.0 / ((2 * n - 1) * (2 * n))) * cosine
    sine = angle * sine
    for _ in range(2):
        sine, cosine = 2.0 * sine * cosine, 1.0 - 2.0 * sine * sine
    return cosine, -sine


def segment_tables_kernel(devices, place_ref, table_ref, twiddle_ref, turn_ref):
    place = place_ref[0]
    points = SIDE * SIDE
    row = lax.broadcasted_iota(jnp.int32, (LANES, LANES), 0)
    lane = lax.broadcasted_iota(jnp.int32, (LANES, LANES), 1)
    line = lax.broadcasted_iota(jnp.int32, (8, LANES), 1)
    whole = unit(row * lane, LANES)
    across = times(unit(row * lane, points // 4), unit(place * row * 4, points * devices))
    down = unit(row, SIDE)
    for g in range(4):
        here = whole
        if g:
            here = times(whole, tuple(x[:1] for x in unit(line * g, SIDE)))
        (cos_high, cos_low), (sin_high, sin_low) = split(here[0]), split(-here[1])
        for k, (cos, sin) in enumerate(((cos_high, sin_high), (cos_low, sin_low))):
            table_ref[k, g, :LANES, :LANES] = cos
            table_ref[k, g, :LANES, LANES:] = sin
            table_ref[k, g, LANES:, :LANES] = -sin
            table_ref[k, g, LANES:, LANES:] = cos
        both = across
        step = down
        if g:
            part_g = times(unit(line * g, points), unit(place * g + 0 * line, points * devices))
            both = times(both, tuple(x[:1] for x in part_g))
            angle = -2.0 * math.pi * g * LANES / points
            step = times(down, (math.cos(angle), math.sin(angle)))
        for j in range(4):
            if j:
                both = times(both, step)
            for part in range(2):
                twiddle_ref[part, g, j] = both[part]
        turn = unit(place * (4 * line + g), SIDE * devices)
        for part in range(2):
            turn_ref[part, g] = turn[part]


def segment_kernel(x_ref, table_ref, twiddle_ref, turn_ref, out_ref, first_ref, second_ref):
    for j in range(4):
        grid = [
            tuple(x_ref[part, pl.ds(SIDE * i + j, LANES, stride=4), :] for part in range(2))
            for i in range(4)
        ]
        for g, pair in enumerate(quarter(grid)):
            for part in range(2):
                high, low = split(pair[part])
                rows, cols = pl.ds(LANES * part, LANES), pl.ds(LANES * j, LANES)
                first_ref[0, g, rows, cols] = high
                first_ref[1, g, rows, cols] = low
    for g in range(4):
        done = dot3((table_ref[0, g], table_ref[1, g]), (first_ref[0, g], first_ref[1, g]))
        grid = []
        for j in range(4):
            cols = slice(LANES * j, LANES * (j + 1))
            both = (twiddle_ref[0, g, j], twiddle_ref[1, g, j])
            grid.append(times((done[:LANES, cols], done[LANES:, cols]), both))
        for h, pair in enumerate(quarter(grid)):
            for part in range(2):
                high, low = split(pair[part])
                rows, cols = pl.ds(LANES * g, LANES), pl.ds(LANES * part, LANES)
                second_ref[0, h, rows, cols] = high
                second_ref[1, h, rows, cols] = low
    for h in range(4):
        done = dot3(
            (second_ref[0, h], second_ref[1, h]), (table_ref[0, h], table_ref[1, h]), ((1,), (1,))
        )
        pair = times((done[:, :LANES], done[:, LANES:]), (turn_ref[0, h, :1], turn_ref[1, h, :1]))
        for part in range(2):
            for upper in range(2):
                out_ref[pl.ds(8 * part + 4 * upper + h, SIDE // 2, stride=16), :] = pair[part][
                    SIDE // 2 * upper : SIDE // 2 * (upper + 1)
                ]


def device_kernel(devices, x_ref, table_ref, out_ref):
    edges = {}
    for block in range(4):
        columns = []
        for e in (2 * block, 2 * block + 1):
            columns.append(
                jnp.concatenate(
                    [x_ref[pl.ds(8 * part + e, devices, stride=16), :] for part in range(2)], axis=0
                )
            )
        x = jnp.concatenate(columns, axis=1)
        done = dot3((table_ref[0], table_ref[1]), split(x))
        for i, e in enumerate((2 * block, 2 * block + 1)):
            values = done[:, LANES * i : LANES * (i + 1)]
            out_ref[pl.ds(e, devices, stride=ROWS), :] = values
            if e % 4 in (0, 3):
                edges[e] = values
    lane = lax.broadcasted_iota(jnp.int32, (devices, LANES), 1)
    row = lax.broadcasted_iota(jnp.int32, (devices, LANES), 0)
    after = jnp.where(lane == 0, edges[0], pltpu.roll(edges[4], 1, 1))
    before = jnp.where(lane == LANES - 1, edges[3], pltpu.roll(edges[7], LANES - 1, 1))
    after = jnp.where(row == devices - 1, 0.0, pltpu.roll(after, devices - 1, 0))
    before = jnp.where(row == 0, 0.0, pltpu.roll(before, 1, 0))
    out_ref[pl.ds(8, devices, stride=ROWS), :] = jnp.where(lane < 2, after, before)


def gain(devices, place, position):
    length = SIDE * SIDE * devices
    centred = place.astype(F32) / devices + position.astype(F32) / length - 0.5
    return length ** (-0.5) * jnp.exp(RATE * centred * centred)


def gram_tables_kernel(index_ref, offset_ref, code_ref, share_ref, entry_ref):
    for odd in range(2):
        rows = pl.ds(odd, LANES, stride=2)
        code = (offset_ref[rows, :] * GAP + index_ref[rows, :]).T
        code_ref[odd] = code
        fraction = (code >> 3).astype(F32) * (1.0 / UPS)
        for w, share in enumerate(shares_of(fraction)[:KEPT]):
            share_ref[w, odd] = share
    line = lax.broadcasted_iota(jnp.int32, (8, LANES), 1) & (UPS - 1)
    for w, share in enumerate(shares_of(line.astype(F32) * (1.0 / UPS))[KEPT:]):
        entry_ref[w] = share


def shares_of(fraction):
    sine = jnp.sin(math.pi * fraction) * (1.0 / math.pi)
    sine = sine * jnp.exp(fraction * fraction * (-0.5 / (SPREAD * SPREAD)))
    at_zero = fraction == 0.0
    shares = [jnp.where(at_zero, 1.0, sine / jnp.where(at_zero, 1.0, fraction))]
    square = fraction * fraction
    up = jnp.exp(fraction * (1.0 / (SPREAD * SPREAD)))
    for w in range(1, HALF, 2):
        odd, even = square - w * w, square - (w + 1) * (w + 1)
        inverse = 1.0 / (odd * even)
        for tap, other in ((w, even), (w + 1, odd)):
            scale = (-1.0) ** tap * math.exp(-0.5 * tap * tap / (SPREAD * SPREAD))
            sine = sine * up
            shares.append((sine * scale) * (other * inverse))
    shares.append(jnp.exp(fraction * (-2.0 / (SPREAD * SPREAD))))
    return shares


def weighted(taps, shares, fraction):
    down = shares[HALF + 1]
    downs = down
    terms = [taps[HALF - 1] * shares[0]]
    for w in range(1, HALF + 1):
        term = taps[HALF - 1 + w] * (fraction + w)
        if w < HALF:
            term = term + (downs * taps[HALF - 1 - w]) * (fraction - w)
        terms.append(term * shares[w])
        downs = downs * down
    while len(terms) > 1:
        terms = [a + b for a, b in zip(terms[::2], terms[1::2])] + terms[len(terms) & ~1 :]
    return terms[0]


def times_kernel(
    devices, place_ref, x_ref, code_ref, share_ref, entry_ref, z_hbm, gram_hbm,
    zs_ref, z_ref, ends_ref, sums, gram_ref, sem, gram_sem,
):
    pad = HALF
    place = place_ref[0]
    length = SIDE * SIDE * devices
    t = lax.broadcasted_iota(jnp.int32, (LANES, LANES), 0)
    line = lax.broadcasted_iota(jnp.int32, (8, LANES), 1)
    for h in range(4):
        begin = SIDE * (4 * line + h)
        base = gain(devices, place, begin)[:1]
        start_c = (place.astype(F32) / devices + begin.astype(F32) / length - 0.5)[:1]
        for g in range(4):
            start = ROWS * LANES * (g % 2) + 4 * (g // 2) + h
            raw = x_ref[pl.ds(start, LANES, stride=ROWS), :]
            du = (4 * t + g).astype(F32) * (1.0 / length)
            x = (du * (2.0 * RATE)) * (start_c + 0.5 * du)
            factor = base + base * (x + 0.5 * x * x)
            zs_ref[h, pl.ds(pad + g, LANES, stride=4), :] = raw * factor
        for block in range(4):
            z_ref[pl.ds(4 * h + block, LANES, stride=16), :] = zs_ref[
                h, pl.ds(pad + LANES * block, LANES), :
            ].T
    copy = pltpu.make_async_copy(z_ref, z_hbm, sem)
    copy.start()
    for g in range(4):
        upper = g // 2
        for side, top, shift in ((0, LANES - 8, 1 + upper), (1, 0, LANES - 1 - upper)):
            start = ROWS * (LANES * (g % 2) + top) + 8
            tile = pltpu.roll(x_ref[pl.ds(start, 8, stride=ROWS), :], shift, 1)
            ends_ref[side, pl.ds(g, 8, stride=4), :] = tile
    lane = lax.broadcasted_iota(jnp.int32, (pad, LANES), 1)
    for h in range(4):
        before = zs_ref[(h - 1) % 4, pl.ds(SIDE, pad), :]
        after = zs_ref[(h + 1) % 4, pl.ds(pad, pad), :]
        if h == 0:
            edge = ends_ref[0, pl.ds(pad, pad), :] * gain(
                devices, place - 1, t[:pad] + (SIDE * SIDE - HALF)
            )
            before = jnp.where(lane == 0, edge, pltpu.roll(before, 1, 1))
        if h == 3:
            edge = ends_ref[1, pl.ds(0, pad), :] * gain(devices, place + 1, t[:pad])
            after = jnp.where(lane == LANES - 1, edge, pltpu.roll(after, LANES - 1, 1))
        zs_ref[h, pl.ds(0, pad), :] = before
        zs_ref[h, pl.ds(pad + SIDE, pad), :] = after
    for h in range(4):

        def body(step, carry, h=h):
            rows = pl.ds(pl.multiple_of(64 * (h % 2) + 8 * step, 8), 8)
            index = code_ref[h // 2, rows, :]
            offset = index >> 3
            fraction = offset.astype(F32) * (1.0 / UPS)
            taps = [
                zs_ref[h, pl.ds(pad + o + 64 * step, 8, stride=8), :]
                for o in range(1 - HALF, HALF + GAP)
            ]
            for bit in (2, 1, 0):
                size = 1 << bit
                chosen = (index >> bit & 1) == 1
                taps = [jnp.where(chosen, b, a) for a, b in zip(taps[:-size], taps[size:])]
            shares = [share_ref[w, h // 2, rows, :] for w in range(KEPT)]
            for w in range(HALF + 2 - KEPT):
                shares.append(jnp.take_along_axis(entry_ref[w], offset, axis=1))
            sums[h // 2, rows, :] = weighted(taps, shares, fraction)
            return carry

        lax.fori_loop(0, 8, body, 0, unroll=4)
    for odd in range(2):
        gram_ref[pl.ds(odd, LANES, stride=2), :] = sums[odd].T
    gram_copy = pltpu.make_async_copy(gram_ref, gram_hbm, gram_sem)
    gram_copy.start()
    copy.wait()
    gram_copy.wait()


def call(kernel, out_shape, specs, scratch=(), flops=0, limit=16, outs="v"):
    spaces = {"s": pltpu.SMEM, "v": pltpu.VMEM, "h": pltpu.HBM}
    out_specs = [pl.BlockSpec(memory_space=spaces[spec]) for spec in outs]
    if len(outs) == 1:
        out_specs = out_specs[0]
    return pl.pallas_call(
        kernel,
        out_shape=out_shape,
        in_specs=[pl.BlockSpec(memory_space=spaces[spec]) for spec in specs],
        out_specs=out_specs,
        scratch_shapes=list(scratch),
        compiler_params=pltpu.CompilerParams(vmem_limit_bytes=limit * MIB),
        cost_estimate=pl.CostEstimate(flops=flops, bytes_accessed=4 * MIB, transcendentals=0),
    )


def struct(shape, kind=F32):
    return jax.ShapeDtypeStruct(tuple(shape), kind)


def segment_tables(devices, place):
    return call(
        functools.partial(segment_tables_kernel, devices),
        (
            struct((2, 4, 2 * LANES, 2 * LANES), BF16),
            struct((2, 4, 4, LANES, LANES)),
            struct((2, 4, 8, LANES)),
        ),
        "s",
        flops=1 << 32,
        outs="vvv",
    )(place)


def segment_transform(samples, tables):
    points = samples.size // 2
    return call(
        segment_kernel,
        struct((points * 2 // LANES, LANES)),
        "vvvv",
        [
            pltpu.VMEM((2, 4, 2 * LANES, SIDE), BF16),
            pltpu.VMEM((2, 4, SIDE, 2 * LANES), BF16),
        ],
        3 * 2 * 8 * SIDE * SIDE * LANES,
    )(samples, *tables)


def device_transform(devices, received):
    return call(
        functools.partial(device_kernel, devices),
        struct((ROWS * devices, LANES)),
        "vv",
        flops=3 * 2 * 2 * devices * received.shape[0] // 2 * LANES,
    )(received, jnp.asarray(device_table(devices)))


def gram_tables(index, offset):
    square = (2, LANES, LANES)
    return call(
        gram_tables_kernel,
        (
            struct(square, jnp.int32),
            struct((KEPT,) + square),
            struct((HALF + 2 - KEPT, 8, LANES)),
        ),
        "vv",
        flops=1 << 26,
        outs="vvv",
    )(index, offset)


def times_block(devices, place, timed, tables):
    rows = SIDE * SIDE // LANES
    return call(
        functools.partial(times_kernel, devices),
        (struct((rows, LANES)), struct((2 * LANES, LANES))),
        "svvvv",
        [
            pltpu.VMEM((4, SIDE + 2 * HALF, LANES), F32),
            pltpu.VMEM((rows, LANES), F32),
            pltpu.VMEM((2, 2 * HALF, LANES), F32),
            pltpu.VMEM((2, LANES, LANES), F32),
            pltpu.VMEM((2 * LANES, LANES), F32),
            pltpu.SemaphoreType.DMA(()),
            pltpu.SemaphoreType.DMA(()),
        ],
        1 << 24,
        outs="hh",
    )(place, timed, *tables)


def local(samples, gram_index, gram_offset):
    inner, outer = lax.axis_size("inner"), lax.axis_size("outer")
    devices = inner * outer
    place = (lax.axis_index("inner") * outer + lax.axis_index("outer")).astype(jnp.int32)
    spot = place.reshape(1)
    points = samples.shape[2]
    rows = gram_index.shape[0] // LANES
    tables = segment_tables(devices, spot)
    tables, index, offset = lax.optimization_barrier(
        (tables, gram_index.reshape(rows, LANES), gram_offset.reshape(rows, LANES))
    )
    weights = gram_tables(index, offset)
    tables, weights = lax.optimization_barrier((tables, weights))
    parts = segment_transform(samples.reshape(2, points // LANES, LANES), tables)
    received = lax.all_to_all(parts.reshape(devices, 16, LANES), AXES, 0, 0, tiled=True)
    real = device_transform(devices, received.reshape(16 * devices, LANES))
    timed = lax.all_to_all(real.reshape(-1), AXES, 0, 0, tiled=True)
    z_field, gram = times_block(
        devices, spot, timed.reshape(ROWS * devices, LANES), weights
    )
    return z_field.reshape(points), gram.reshape(-1)


def solution(mesh):
    return jax.shard_map(
        local,
        mesh=mesh,
        in_specs=(P(None, AXES, None), P(AXES), P(AXES)),
        out_specs=(P(AXES), P(AXES)),
        check_vma=False,
    )
```

```python
import functools
import math

import jax
import jax.numpy as jnp
import numpy as np
from jax import lax
from jax.experimental import pallas as pl
from jax.experimental.pallas import tpu as pltpu
from jax.sharding import PartitionSpec as P

GAP = 8
HALF = 16
UPS = 32
RATE = 4.0
SPREAD = HALF / 2.0
SIDE = 512
LANES = 128
KEPT = 13
ROWS = 9
AXES = ("inner", "outer")
F32 = jnp.float32
BF16 = jnp.bfloat16
MIB = 1 << 20


def halves(table):
    high = table.astype(jnp.bfloat16)
    low = (table - high.astype(np.float64)).astype(jnp.bfloat16)
    return np.stack([high, low])


def device_table(devices):
    n = np.arange(devices // 2)
    tables = []
    for g in range(2):
        angle = 2.0 * np.pi * ((2 * n[:, None] + g) * n[None, :] % devices) / devices
        tables.append(np.concatenate([np.cos(angle), np.sin(angle)], axis=1))
    return halves(np.stack(tables))


def split(x):
    high = x.astype(BF16)
    return high, (x - high.astype(F32)).astype(BF16)


def dot(a, b, dims):
    return lax.dot_general(a, b, (dims, ((), ())), preferred_element_type=F32)


def dot3(a, b, dims=((1,), (0,))):
    (a_high, a_low), (b_high, b_low) = a, b
    return dot(a_high, b_high, dims) + (dot(a_high, b_low, dims) + dot(a_low, b_high, dims))


def quarter(parts):
    (r0, i0), (r1, i1), (r2, i2), (r3, i3) = parts
    ar, ai, br, bi = r0 + r2, i0 + i2, r0 - r2, i0 - i2
    cr, ci, er, ei = r1 + r3, i1 + i3, r1 - r3, i1 - i3
    return [(ar + cr, ai + ci), (br + ei, bi - er), (ar - cr, ai - ci), (br - ei, bi + er)]


def times(a, b):
    return a[0] * b[0] - a[1] * b[1], a[0] * b[1] + a[1] * b[0]


def unit(count, period):
    half = period // 2
    near = ((count + half) & (period - 1)) - half
    angle = near.astype(F32) * (0.5 * math.pi / period)
    square = angle * angle
    sine, cosine = 1.0, 1.0
    for n in (4, 3, 2, 1):
        sine = 1.0 - square * (1.0 / ((2 * n) * (2 * n + 1))) * sine
    for n in (5, 4, 3, 2, 1):
        cosine = 1.0 - square * (1.0 / ((2 * n - 1) * (2 * n))) * cosine
    sine = angle * sine
    for _ in range(2):
        sine, cosine = 2.0 * sine * cosine, 1.0 - 2.0 * sine * sine
    return cosine, -sine


def segment_tables_kernel(devices, place_ref, table_ref, twiddle_ref, turn_ref):
    place = place_ref[0]
    points = SIDE * SIDE
    row = lax.broadcasted_iota(jnp.int32, (LANES, LANES), 0)
    lane = lax.broadcasted_iota(jnp.int32, (LANES, LANES), 1)
    line = lax.broadcasted_iota(jnp.int32, (8, LANES), 1)
    whole = unit(row * lane, LANES)
    across = times(unit(row * lane, points // 4), unit(place * row * 4, points * devices))
    down = unit(row, SIDE)
    for g in range(4):
        here = whole
        if g:
            here = times(whole, tuple(x[:1] for x in unit(line * g, SIDE)))
        (cos_high, cos_low), (sin_high, sin_low) = split(here[0]), split(-here[1])
        for k, (cos, sin) in enumerate(((cos_high, sin_high), (cos_low, sin_low))):
            table_ref[k, g, :LANES, :LANES] = cos
            table_ref[k, g, :LANES, LANES:] = sin
            table_ref[k, g, LANES:, :LANES] = -sin
            table_ref[k, g, LANES:, LANES:] = cos
        both = across
        step = down
        if g:
            part_g = times(unit(line * g, points), unit(place * g + 0 * line, points * devices))
            both = times(both, tuple(x[:1] for x in part_g))
            angle = -2.0 * math.pi * g * LANES / points
            step = times(down, (math.cos(angle), math.sin(angle)))
        for j in range(4):
            if j:
                both = times(both, step)
            for part in range(2):
                twiddle_ref[part, g, j] = both[part]
        turn = unit(place * (4 * line + g), SIDE * devices)
        for part in range(2):
            turn_ref[part, g] = turn[part]


def segment_kernel(x_ref, table_ref, twiddle_ref, turn_ref, out_ref, first_ref, second_ref):
    for j in range(4):
        grid = [
            tuple(x_ref[part, pl.ds(SIDE * i + j, LANES, stride=4), :] for part in range(2))
            for i in range(4)
        ]
        for g, pair in enumerate(quarter(grid)):
            for part in range(2):
                high, low = split(pair[part])
                rows, cols = pl.ds(LANES * part, LANES), pl.ds(LANES * j, LANES)
                first_ref[0, g, rows, cols] = high
                first_ref[1, g, rows, cols] = low
    for g in range(4):
        done = dot3((table_ref[0, g], table_ref[1, g]), (first_ref[0, g], first_ref[1, g]))
        grid = []
        for j in range(4):
            cols = slice(LANES * j, LANES * (j + 1))
            both = (twiddle_ref[0, g, j], twiddle_ref[1, g, j])
            grid.append(times((done[:LANES, cols], done[LANES:, cols]), both))
        for h, pair in enumerate(quarter(grid)):
            for part in range(2):
                high, low = split(pair[part])
                rows, cols = pl.ds(LANES * g, LANES), pl.ds(LANES * part, LANES)
                second_ref[0, h, rows, cols] = high
                second_ref[1, h, rows, cols] = low
    for h in range(4):
        done = dot3(
            (second_ref[0, h], second_ref[1, h]), (table_ref[0, h], table_ref[1, h]), ((1,), (1,))
        )
        pair = times((done[:, :LANES], done[:, LANES:]), (turn_ref[0, h, :1], turn_ref[1, h, :1]))
        for part in range(2):
            for upper in range(2):
                out_ref[pl.ds(8 * part + 4 * upper + h, SIDE // 2, stride=16), :] = pair[part][
                    SIDE // 2 * upper : SIDE // 2 * (upper + 1)
                ]


def device_kernel(devices, x_ref, table_ref, out_ref):
    count = devices // 2
    edges = {}
    for block in range(4):
        columns = ([], [])
        for e in (2 * block, 2 * block + 1):
            pairs = [
                [x_ref[pl.ds(16 * count * i + 8 * part + e, count, stride=16), :] for i in range(2)]
                for part in range(2)
            ]
            columns[0].append(jnp.concatenate([low + high for low, high in pairs], axis=0))
            columns[1].append(jnp.concatenate([low - high for low, high in pairs], axis=0))
        for g in range(2):
            x = jnp.concatenate(columns[g], axis=1)
            done = dot3((table_ref[0, g], table_ref[1, g]), split(x))
            for i, e in enumerate((2 * block, 2 * block + 1)):
                values = done[:, LANES * i : LANES * (i + 1)]
                out_ref[pl.ds(ROWS * g + e, count, stride=2 * ROWS), :] = values
                if e % 4 in (0, 3):
                    edges[e, g] = values
    lane = lax.broadcasted_iota(jnp.int32, (count, LANES), 1)
    row = lax.broadcasted_iota(jnp.int32, (count, LANES), 0)
    after, before = [], []
    for g in range(2):
        after.append(jnp.where(lane == 0, edges[0, g], pltpu.roll(edges[4, g], 1, 1)))
        before.append(
            jnp.where(lane == LANES - 1, edges[3, g], pltpu.roll(edges[7, g], LANES - 1, 1))
        )
    later = jnp.where(row == count - 1, 0.0, pltpu.roll(after[0], count - 1, 0))
    earlier = jnp.where(row == 0, 0.0, pltpu.roll(before[1], 1, 0))
    for g, (up, down) in enumerate(((after[1], earlier), (later, before[0]))):
        out_ref[pl.ds(ROWS * g + 8, count, stride=2 * ROWS), :] = jnp.where(lane < 2, up, down)


def gain(devices, place, position):
    length = SIDE * SIDE * devices
    centred = place.astype(F32) / devices + position.astype(F32) / length - 0.5
    return length ** (-0.5) * jnp.exp(RATE * centred * centred)


def gram_tables_kernel(index_ref, offset_ref, code_ref, share_ref, entry_ref):
    for odd in range(2):
        rows = pl.ds(odd, LANES, stride=2)
        code = (offset_ref[rows, :] * GAP + index_ref[rows, :]).T
        code_ref[odd] = code
        fraction = (code >> 3).astype(F32) * (1.0 / UPS)
        for w, share in enumerate(shares_of(fraction)[:KEPT]):
            share_ref[w, odd] = share
    line = lax.broadcasted_iota(jnp.int32, (8, LANES), 1) & (UPS - 1)
    for w, share in enumerate(shares_of(line.astype(F32) * (1.0 / UPS))[KEPT:]):
        entry_ref[w] = share


def shares_of(fraction):
    sine = jnp.sin(math.pi * fraction) * (1.0 / math.pi)
    sine = sine * jnp.exp(fraction * fraction * (-0.5 / (SPREAD * SPREAD)))
    at_zero = fraction == 0.0
    shares = [jnp.where(at_zero, 1.0, sine / jnp.where(at_zero, 1.0, fraction))]
    square = fraction * fraction
    up = jnp.exp(fraction * (1.0 / (SPREAD * SPREAD)))
    for w in range(1, HALF, 2):
        odd, even = square - w * w, square - (w + 1) * (w + 1)
        inverse = 1.0 / (odd * even)
        for tap, other in ((w, even), (w + 1, odd)):
            scale = (-1.0) ** tap * math.exp(-0.5 * tap * tap / (SPREAD * SPREAD))
            sine = sine * up
            shares.append((sine * scale) * (other * inverse))
    shares.append(jnp.exp(fraction * (-2.0 / (SPREAD * SPREAD))))
    return shares


def weighted(taps, shares, fraction):
    down = shares[HALF + 1]
    downs = down
    terms = [taps[HALF - 1] * shares[0]]
    for w in range(1, HALF + 1):
        term = taps[HALF - 1 + w] * (fraction + w)
        if w < HALF:
            term = term + (downs * taps[HALF - 1 - w]) * (fraction - w)
        terms.append(term * shares[w])
        downs = downs * down
    while len(terms) > 1:
        terms = [a + b for a, b in zip(terms[::2], terms[1::2])] + terms[len(terms) & ~1 :]
    return terms[0]


def times_kernel(
    devices, place_ref, x_ref, code_ref, share_ref, entry_ref, z_hbm, gram_hbm,
    zs_ref, z_ref, ends_ref, sums, gram_ref, sem, gram_sem,
):
    pad = HALF
    place = place_ref[0]
    length = SIDE * SIDE * devices
    t = lax.broadcasted_iota(jnp.int32, (LANES, LANES), 0)
    line = lax.broadcasted_iota(jnp.int32, (8, LANES), 1)
    for h in range(4):
        begin = SIDE * (4 * line + h)
        base = gain(devices, place, begin)[:1]
        start_c = (place.astype(F32) / devices + begin.astype(F32) / length - 0.5)[:1]
        for g in range(4):
            start = ROWS * LANES * (g % 2) + 4 * (g // 2) + h
            raw = x_ref[pl.ds(start, LANES, stride=ROWS), :]
            du = (4 * t + g).astype(F32) * (1.0 / length)
            x = (du * (2.0 * RATE)) * (start_c + 0.5 * du)
            factor = base + base * (x + 0.5 * x * x)
            zs_ref[h, pl.ds(pad + g, LANES, stride=4), :] = raw * factor
        for block in range(4):
            z_ref[pl.ds(4 * h + block, LANES, stride=16), :] = zs_ref[
                h, pl.ds(pad + LANES * block, LANES), :
            ].T
    copy = pltpu.make_async_copy(z_ref, z_hbm, sem)
    copy.start()
    for g in range(4):
        upper = g // 2
        for side, top, shift in ((0, LANES - 8, 1 + upper), (1, 0, LANES - 1 - upper)):
            start = ROWS * (LANES * (g % 2) + top) + 8
            tile = pltpu.roll(x_ref[pl.ds(start, 8, stride=ROWS), :], shift, 1)
            ends_ref[side, pl.ds(g, 8, stride=4), :] = tile
    lane = lax.broadcasted_iota(jnp.int32, (pad, LANES), 1)
    for h in range(4):
        before = zs_ref[(h - 1) % 4, pl.ds(SIDE, pad), :]
        after = zs_ref[(h + 1) % 4, pl.ds(pad, pad), :]
        if h == 0:
            edge = ends_ref[0, pl.ds(pad, pad), :] * gain(
                devices, place - 1, t[:pad] + (SIDE * SIDE - HALF)
            )
            before = jnp.where(lane == 0, edge, pltpu.roll(before, 1, 1))
        if h == 3:
            edge = ends_ref[1, pl.ds(0, pad), :] * gain(devices, place + 1, t[:pad])
            after = jnp.where(lane == LANES - 1, edge, pltpu.roll(after, LANES - 1, 1))
        zs_ref[h, pl.ds(0, pad), :] = before
        zs_ref[h, pl.ds(pad + SIDE, pad), :] = after
    for h in range(4):

        def body(step, carry, h=h):
            rows = pl.ds(pl.multiple_of(64 * (h % 2) + 8 * step, 8), 8)
            index = code_ref[h // 2, rows, :]
            offset = index >> 3
            fraction = offset.astype(F32) * (1.0 / UPS)
            taps = [
                zs_ref[h, pl.ds(pad + o + 64 * step, 8, stride=8), :]
                for o in range(1 - HALF, HALF + GAP)
            ]
            for bit in (2, 1, 0):
                size = 1 << bit
                chosen = (index >> bit & 1) == 1
                taps = [jnp.where(chosen, b, a) for a, b in zip(taps[:-size], taps[size:])]
            shares = [share_ref[w, h // 2, rows, :] for w in range(KEPT)]
            for w in range(HALF + 2 - KEPT):
                shares.append(jnp.take_along_axis(entry_ref[w], offset, axis=1))
            sums[h // 2, rows, :] = weighted(taps, shares, fraction)
            return carry

        lax.fori_loop(0, 8, body, 0, unroll=4)
    for odd in range(2):
        gram_ref[pl.ds(odd, LANES, stride=2), :] = sums[odd].T
    gram_copy = pltpu.make_async_copy(gram_ref, gram_hbm, gram_sem)
    gram_copy.start()
    copy.wait()
    gram_copy.wait()


def call(kernel, out_shape, specs, scratch=(), flops=0, limit=16, outs="v"):
    spaces = {"s": pltpu.SMEM, "v": pltpu.VMEM, "h": pltpu.HBM}
    out_specs = [pl.BlockSpec(memory_space=spaces[spec]) for spec in outs]
    if len(outs) == 1:
        out_specs = out_specs[0]
    return pl.pallas_call(
        kernel,
        out_shape=out_shape,
        in_specs=[pl.BlockSpec(memory_space=spaces[spec]) for spec in specs],
        out_specs=out_specs,
        scratch_shapes=list(scratch),
        compiler_params=pltpu.CompilerParams(vmem_limit_bytes=limit * MIB),
        cost_estimate=pl.CostEstimate(flops=flops, bytes_accessed=4 * MIB, transcendentals=0),
    )


def struct(shape, kind=F32):
    return jax.ShapeDtypeStruct(tuple(shape), kind)


def segment_tables(devices, place):
    return call(
        functools.partial(segment_tables_kernel, devices),
        (
            struct((2, 4, 2 * LANES, 2 * LANES), BF16),
            struct((2, 4, 4, LANES, LANES)),
            struct((2, 4, 8, LANES)),
        ),
        "s",
        flops=1 << 32,
        outs="vvv",
    )(place)


def segment_transform(samples, tables):
    points = samples.size // 2
    return call(
        segment_kernel,
        struct((points * 2 // LANES, LANES)),
        "vvvv",
        [
            pltpu.VMEM((2, 4, 2 * LANES, SIDE), BF16),
            pltpu.VMEM((2, 4, SIDE, 2 * LANES), BF16),
        ],
        3 * 2 * 8 * SIDE * SIDE * LANES,
    )(samples, *tables)


def device_transform(devices, received):
    return call(
        functools.partial(device_kernel, devices),
        struct((ROWS * devices, LANES)),
        "vv",
        flops=3 * 2 * 2 * devices * received.shape[0] // 2 * LANES,
    )(received, jnp.asarray(device_table(devices)))


def gram_tables(index, offset):
    square = (2, LANES, LANES)
    return call(
        gram_tables_kernel,
        (
            struct(square, jnp.int32),
            struct((KEPT,) + square),
            struct((HALF + 2 - KEPT, 8, LANES)),
        ),
        "vv",
        flops=1 << 26,
        outs="vvv",
    )(index, offset)


def times_block(devices, place, timed, tables):
    rows = SIDE * SIDE // LANES
    return call(
        functools.partial(times_kernel, devices),
        (struct((rows, LANES)), struct((2 * LANES, LANES))),
        "svvvv",
        [
            pltpu.VMEM((4, SIDE + 2 * HALF, LANES), F32),
            pltpu.VMEM((rows, LANES), F32),
            pltpu.VMEM((2, 2 * HALF, LANES), F32),
            pltpu.VMEM((2, LANES, LANES), F32),
            pltpu.VMEM((2 * LANES, LANES), F32),
            pltpu.SemaphoreType.DMA(()),
            pltpu.SemaphoreType.DMA(()),
        ],
        1 << 24,
        outs="hh",
    )(place, timed, *tables)


def local(samples, gram_index, gram_offset):
    inner, outer = lax.axis_size("inner"), lax.axis_size("outer")
    devices = inner * outer
    place = (lax.axis_index("inner") * outer + lax.axis_index("outer")).astype(jnp.int32)
    spot = place.reshape(1)
    points = samples.shape[2]
    rows = gram_index.shape[0] // LANES
    tables = segment_tables(devices, spot)
    tables, index, offset = lax.optimization_barrier(
        (tables, gram_index.reshape(rows, LANES), gram_offset.reshape(rows, LANES))
    )
    weights = gram_tables(index, offset)
    tables, weights = lax.optimization_barrier((tables, weights))
    parts = segment_transform(samples.reshape(2, points // LANES, LANES), tables)
    received = lax.all_to_all(parts.reshape(devices, 16, LANES), AXES, 0, 0, tiled=True)
    real = device_transform(devices, received.reshape(16 * devices, LANES))
    timed = lax.all_to_all(real.reshape(-1), AXES, 0, 0, tiled=True)
    z_field, gram = times_block(
        devices, spot, timed.reshape(ROWS * devices, LANES), weights
    )
    return z_field.reshape(points), gram.reshape(-1)


def solution(mesh):
    return jax.shard_map(
        local,
        mesh=mesh,
        in_specs=(P(None, AXES, None), P(AXES), P(AXES)),
        out_specs=(P(AXES), P(AXES)),
        check_vma=False,
    )
```

```python
import functools
import math

import jax
import jax.numpy as jnp
import numpy as np
from jax import lax
from jax.experimental import pallas as pl
from jax.experimental.pallas import tpu as pltpu
from jax.sharding import PartitionSpec as P

GAP = 8
HALF = 16
UPS = 32
RATE = 4.0
SPREAD = HALF / 2.0
SIDE = 512
LANES = 128
KEPT = 9
ROWS = 9
AXES = ("inner", "outer")
F32 = jnp.float32
BF16 = jnp.bfloat16
MIB = 1 << 20


def halves(table):
    high = table.astype(jnp.bfloat16)
    low = (table - high.astype(np.float64)).astype(jnp.bfloat16)
    return np.stack([high, low])


def device_table(devices):
    n = np.arange(devices // 2)
    tables = []
    for g in range(2):
        angle = 2.0 * np.pi * ((2 * n[:, None] + g) * n[None, :] % devices) / devices
        tables.append(np.concatenate([np.cos(angle), np.sin(angle)], axis=1))
    return halves(np.stack(tables))


def split(x):
    high = x.astype(BF16)
    return high, (x - high.astype(F32)).astype(BF16)


def dot(a, b, dims):
    return lax.dot_general(a, b, (dims, ((), ())), preferred_element_type=F32)


def dot3(a, b, dims=((1,), (0,))):
    (a_high, a_low), (b_high, b_low) = a, b
    return dot(a_high, b_high, dims) + (dot(a_high, b_low, dims) + dot(a_low, b_high, dims))


def quarter(parts):
    (r0, i0), (r1, i1), (r2, i2), (r3, i3) = parts
    ar, ai, br, bi = r0 + r2, i0 + i2, r0 - r2, i0 - i2
    cr, ci, er, ei = r1 + r3, i1 + i3, r1 - r3, i1 - i3
    return [(ar + cr, ai + ci), (br + ei, bi - er), (ar - cr, ai - ci), (br - ei, bi + er)]


def times(a, b):
    return a[0] * b[0] - a[1] * b[1], a[0] * b[1] + a[1] * b[0]


def unit(count, period):
    half = period // 2
    near = ((count + half) & (period - 1)) - half
    angle = near.astype(F32) * (0.5 * math.pi / period)
    square = angle * angle
    sine, cosine = 1.0, 1.0
    for n in (4, 3, 2, 1):
        sine = 1.0 - square * (1.0 / ((2 * n) * (2 * n + 1))) * sine
    for n in (5, 4, 3, 2, 1):
        cosine = 1.0 - square * (1.0 / ((2 * n - 1) * (2 * n))) * cosine
    sine = angle * sine
    for _ in range(2):
        sine, cosine = 2.0 * sine * cosine, 1.0 - 2.0 * sine * sine
    return cosine, -sine


def segment_tables_kernel(devices, place_ref, table_ref, twiddle_ref, turn_ref):
    place = place_ref[0]
    points = SIDE * SIDE
    row = lax.broadcasted_iota(jnp.int32, (LANES, LANES), 0)
    lane = lax.broadcasted_iota(jnp.int32, (LANES, LANES), 1)
    line = lax.broadcasted_iota(jnp.int32, (8, LANES), 1)
    whole = unit(row * lane, LANES)
    across = times(unit(row * lane, points // 4), unit(place * row * 4, points * devices))
    down = unit(row, SIDE)
    for g in range(4):
        here = whole
        if g:
            here = times(whole, tuple(x[:1] for x in unit(line * g, SIDE)))
        (cos_high, cos_low), (sin_high, sin_low) = split(here[0]), split(-here[1])
        for k, (cos, sin) in enumerate(((cos_high, sin_high), (cos_low, sin_low))):
            table_ref[k, g, :LANES, :LANES] = cos
            table_ref[k, g, :LANES, LANES:] = sin
            table_ref[k, g, LANES:, :LANES] = -sin
            table_ref[k, g, LANES:, LANES:] = cos
        both = across
        step = down
        if g:
            part_g = times(unit(line * g, points), unit(place * g + 0 * line, points * devices))
            both = times(both, tuple(x[:1] for x in part_g))
            angle = -2.0 * math.pi * g * LANES / points
            step = times(down, (math.cos(angle), math.sin(angle)))
        for j in range(4):
            if j:
                both = times(both, step)
            for part in range(2):
                twiddle_ref[part, g, j] = both[part]
        turn = unit(place * (4 * line + g), SIDE * devices)
        for part in range(2):
            turn_ref[part, g] = turn[part]


def segment_kernel(x_ref, table_ref, twiddle_ref, turn_ref, out_ref, first_ref, second_ref):
    for j in range(4):
        grid = [
            tuple(x_ref[part, pl.ds(SIDE * i + j, LANES, stride=4), :] for part in range(2))
            for i in range(4)
        ]
        for g, pair in enumerate(quarter(grid)):
            for part in range(2):
                high, low = split(pair[part])
                rows, cols = pl.ds(LANES * part, LANES), pl.ds(LANES * j, LANES)
                first_ref[0, g, rows, cols] = high
                first_ref[1, g, rows, cols] = low
    for g in range(4):
        done = dot3((table_ref[0, g], table_ref[1, g]), (first_ref[0, g], first_ref[1, g]))
        grid = []
        for j in range(4):
            cols = slice(LANES * j, LANES * (j + 1))
            both = (twiddle_ref[0, g, j], twiddle_ref[1, g, j])
            grid.append(times((done[:LANES, cols], done[LANES:, cols]), both))
        for h, pair in enumerate(quarter(grid)):
            for part in range(2):
                high, low = split(pair[part])
                rows, cols = pl.ds(LANES * g, LANES), pl.ds(LANES * part, LANES)
                second_ref[0, h, rows, cols] = high
                second_ref[1, h, rows, cols] = low
    for h in range(4):
        done = dot3(
            (second_ref[0, h], second_ref[1, h]), (table_ref[0, h], table_ref[1, h]), ((1,), (1,))
        )
        pair = times((done[:, :LANES], done[:, LANES:]), (turn_ref[0, h, :1], turn_ref[1, h, :1]))
        for part in range(2):
            for upper in range(2):
                out_ref[pl.ds(8 * part + 4 * upper + h, SIDE // 2, stride=16), :] = pair[part][
                    SIDE // 2 * upper : SIDE // 2 * (upper + 1)
                ]


def device_kernel(devices, x_ref, table_ref, out_ref):
    count = devices // 2
    edges = {}
    for block in range(4):
        columns = ([], [])
        for e in (2 * block, 2 * block + 1):
            pairs = [
                [x_ref[pl.ds(16 * count * i + 8 * part + e, count, stride=16), :] for i in range(2)]
                for part in range(2)
            ]
            columns[0].append(jnp.concatenate([low + high for low, high in pairs], axis=0))
            columns[1].append(jnp.concatenate([low - high for low, high in pairs], axis=0))
        for g in range(2):
            x = jnp.concatenate(columns[g], axis=1)
            done = dot3((table_ref[0, g], table_ref[1, g]), split(x))
            for i, e in enumerate((2 * block, 2 * block + 1)):
                values = done[:, LANES * i : LANES * (i + 1)]
                out_ref[pl.ds(ROWS * g + e, count, stride=2 * ROWS), :] = values
                if e % 4 in (0, 3):
                    edges[e, g] = values
    lane = lax.broadcasted_iota(jnp.int32, (count, LANES), 1)
    row = lax.broadcasted_iota(jnp.int32, (count, LANES), 0)
    after, before = [], []
    for g in range(2):
        after.append(jnp.where(lane == 0, edges[0, g], pltpu.roll(edges[4, g], 1, 1)))
        before.append(
            jnp.where(lane == LANES - 1, edges[3, g], pltpu.roll(edges[7, g], LANES - 1, 1))
        )
    later = jnp.where(row == count - 1, 0.0, pltpu.roll(after[0], count - 1, 0))
    earlier = jnp.where(row == 0, 0.0, pltpu.roll(before[1], 1, 0))
    for g, (up, down) in enumerate(((after[1], earlier), (later, before[0]))):
        out_ref[pl.ds(ROWS * g + 8, count, stride=2 * ROWS), :] = jnp.where(lane < 2, up, down)


def gain(devices, place, position):
    length = SIDE * SIDE * devices
    centred = place.astype(F32) / devices + position.astype(F32) / length - 0.5
    return length ** (-0.5) * jnp.exp(RATE * centred * centred)


def gram_tables_kernel(index_ref, offset_ref, code_ref, share_ref, entry_ref):
    for odd in range(2):
        rows = pl.ds(odd, LANES, stride=2)
        code = (offset_ref[rows, :] * GAP + index_ref[rows, :]).T
        code_ref[odd] = code
        fraction = (code >> 3).astype(F32) * (1.0 / UPS)
        for w, share in enumerate(shares_of(fraction)[:KEPT]):
            share_ref[w, odd] = share
    line = lax.broadcasted_iota(jnp.int32, (8, LANES), 1) & (UPS - 1)
    for w, share in enumerate(shares_of(line.astype(F32) * (1.0 / UPS))[KEPT:]):
        entry_ref[w] = share


def shares_of(fraction):
    sine = jnp.sin(math.pi * fraction) * (1.0 / math.pi)
    sine = sine * jnp.exp(fraction * fraction * (-0.5 / (SPREAD * SPREAD)))
    at_zero = fraction == 0.0
    shares = [jnp.where(at_zero, 1.0, sine / jnp.where(at_zero, 1.0, fraction))]
    square = fraction * fraction
    up = jnp.exp(fraction * (1.0 / (SPREAD * SPREAD)))
    for w in range(1, HALF, 2):
        odd, even = square - w * w, square - (w + 1) * (w + 1)
        inverse = 1.0 / (odd * even)
        for tap, other in ((w, even), (w + 1, odd)):
            scale = (-1.0) ** tap * math.exp(-0.5 * tap * tap / (SPREAD * SPREAD))
            sine = sine * up
            shares.append((sine * scale) * (other * inverse))
    shares.append(jnp.exp(fraction * (-2.0 / (SPREAD * SPREAD))))
    return shares


def weighted(taps, shares, fraction):
    down = shares[HALF + 1]
    downs = down
    terms = [taps[HALF - 1] * shares[0]]
    for w in range(1, HALF + 1):
        term = taps[HALF - 1 + w] * (fraction + w)
        if w < HALF:
            term = term + (downs * taps[HALF - 1 - w]) * (fraction - w)
        terms.append(term * shares[w])
        downs = downs * down
    while len(terms) > 1:
        terms = [a + b for a, b in zip(terms[::2], terms[1::2])] + terms[len(terms) & ~1 :]
    return terms[0]


def times_kernel(
    devices, place_ref, x_ref, code_ref, share_ref, entry_ref, z_hbm, gram_hbm,
    zs_ref, z_ref, ends_ref, sums, gram_ref, sem, gram_sem,
):
    pad = HALF
    place = place_ref[0]
    length = SIDE * SIDE * devices
    t = lax.broadcasted_iota(jnp.int32, (LANES, LANES), 0)
    line = lax.broadcasted_iota(jnp.int32, (8, LANES), 1)
    for h in range(4):
        begin = SIDE * (4 * line + h)
        base = gain(devices, place, begin)[:1]
        start_c = (place.astype(F32) / devices + begin.astype(F32) / length - 0.5)[:1]
        for g in range(4):
            start = ROWS * LANES * (g % 2) + 4 * (g // 2) + h
            raw = x_ref[pl.ds(start, LANES, stride=ROWS), :]
            du = (4 * t + g).astype(F32) * (1.0 / length)
            x = (du * (2.0 * RATE)) * (start_c + 0.5 * du)
            factor = base + base * (x + 0.5 * x * x)
            zs_ref[h, pl.ds(pad + g, LANES, stride=4), :] = raw * factor
        for block in range(4):
            z_ref[pl.ds(4 * h + block, LANES, stride=16), :] = zs_ref[
                h, pl.ds(pad + LANES * block, LANES), :
            ].T
    copy = pltpu.make_async_copy(z_ref, z_hbm, sem)
    copy.start()
    for g in range(4):
        upper = g // 2
        for side, top, shift in ((0, LANES - 8, 1 + upper), (1, 0, LANES - 1 - upper)):
            start = ROWS * (LANES * (g % 2) + top) + 8
            tile = pltpu.roll(x_ref[pl.ds(start, 8, stride=ROWS), :], shift, 1)
            ends_ref[side, pl.ds(g, 8, stride=4), :] = tile
    lane = lax.broadcasted_iota(jnp.int32, (pad, LANES), 1)
    for h in range(4):
        before = zs_ref[(h - 1) % 4, pl.ds(SIDE, pad), :]
        after = zs_ref[(h + 1) % 4, pl.ds(pad, pad), :]
        if h == 0:
            edge = ends_ref[0, pl.ds(pad, pad), :] * gain(
                devices, place - 1, t[:pad] + (SIDE * SIDE - HALF)
            )
            before = jnp.where(lane == 0, edge, pltpu.roll(before, 1, 1))
        if h == 3:
            edge = ends_ref[1, pl.ds(0, pad), :] * gain(devices, place + 1, t[:pad])
            after = jnp.where(lane == LANES - 1, edge, pltpu.roll(after, LANES - 1, 1))
        zs_ref[h, pl.ds(0, pad), :] = before
        zs_ref[h, pl.ds(pad + SIDE, pad), :] = after
    for h in range(4):

        def body(step, carry, h=h):
            rows = pl.ds(pl.multiple_of(64 * (h % 2) + 8 * step, 8), 8)
            index = code_ref[h // 2, rows, :]
            offset = index >> 3
            fraction = offset.astype(F32) * (1.0 / UPS)
            taps = [
                zs_ref[h, pl.ds(pad + o + 64 * step, 8, stride=8), :]
                for o in range(1 - HALF, HALF + GAP)
            ]
            for bit in (2, 1, 0):
                size = 1 << bit
                chosen = (index >> bit & 1) == 1
                taps = [jnp.where(chosen, b, a) for a, b in zip(taps[:-size], taps[size:])]
            shares = [share_ref[w, h // 2, rows, :] for w in range(KEPT)]
            for w in range(HALF + 2 - KEPT):
                shares.append(jnp.take_along_axis(entry_ref[w], offset, axis=1))
            sums[h // 2, rows, :] = weighted(taps, shares, fraction)
            return carry

        lax.fori_loop(0, 8, body, 0, unroll=4)
    for odd in range(2):
        gram_ref[pl.ds(odd, LANES, stride=2), :] = sums[odd].T
    gram_copy = pltpu.make_async_copy(gram_ref, gram_hbm, gram_sem)
    gram_copy.start()
    copy.wait()
    gram_copy.wait()


def call(kernel, out_shape, specs, scratch=(), flops=0, limit=16, outs="v"):
    spaces = {"s": pltpu.SMEM, "v": pltpu.VMEM, "h": pltpu.HBM}
    out_specs = [pl.BlockSpec(memory_space=spaces[spec]) for spec in outs]
    if len(outs) == 1:
        out_specs = out_specs[0]
    return pl.pallas_call(
        kernel,
        out_shape=out_shape,
        in_specs=[pl.BlockSpec(memory_space=spaces[spec]) for spec in specs],
        out_specs=out_specs,
        scratch_shapes=list(scratch),
        compiler_params=pltpu.CompilerParams(vmem_limit_bytes=limit * MIB),
        cost_estimate=pl.CostEstimate(flops=flops, bytes_accessed=4 * MIB, transcendentals=0),
    )


def struct(shape, kind=F32):
    return jax.ShapeDtypeStruct(tuple(shape), kind)


def segment_tables(devices, place):
    return call(
        functools.partial(segment_tables_kernel, devices),
        (
            struct((2, 4, 2 * LANES, 2 * LANES), BF16),
            struct((2, 4, 4, LANES, LANES)),
            struct((2, 4, 8, LANES)),
        ),
        "s",
        flops=1 << 32,
        outs="vvv",
    )(place)


def segment_transform(samples, tables):
    points = samples.size // 2
    return call(
        segment_kernel,
        struct((points * 2 // LANES, LANES)),
        "vvvv",
        [
            pltpu.VMEM((2, 4, 2 * LANES, SIDE), BF16),
            pltpu.VMEM((2, 4, SIDE, 2 * LANES), BF16),
        ],
        3 * 2 * 8 * SIDE * SIDE * LANES,
    )(samples, *tables)


def device_transform(devices, received):
    return call(
        functools.partial(device_kernel, devices),
        struct((ROWS * devices, LANES)),
        "vv",
        flops=3 * 2 * 2 * devices * received.shape[0] // 2 * LANES,
    )(received, jnp.asarray(device_table(devices)))


def gram_tables(index, offset):
    square = (2, LANES, LANES)
    return call(
        gram_tables_kernel,
        (
            struct(square, jnp.int32),
            struct((KEPT,) + square),
            struct((HALF + 2 - KEPT, 8, LANES)),
        ),
        "vv",
        flops=1 << 26,
        outs="vvv",
    )(index, offset)


def times_block(devices, place, timed, tables):
    rows = SIDE * SIDE // LANES
    return call(
        functools.partial(times_kernel, devices),
        (struct((rows, LANES)), struct((2 * LANES, LANES))),
        "svvvv",
        [
            pltpu.VMEM((4, SIDE + 2 * HALF, LANES), F32),
            pltpu.VMEM((rows, LANES), F32),
            pltpu.VMEM((2, 2 * HALF, LANES), F32),
            pltpu.VMEM((2, LANES, LANES), F32),
            pltpu.VMEM((2 * LANES, LANES), F32),
            pltpu.SemaphoreType.DMA(()),
            pltpu.SemaphoreType.DMA(()),
        ],
        1 << 24,
        outs="hh",
    )(place, timed, *tables)


def local(samples, gram_index, gram_offset):
    inner, outer = lax.axis_size("inner"), lax.axis_size("outer")
    devices = inner * outer
    place = (lax.axis_index("inner") * outer + lax.axis_index("outer")).astype(jnp.int32)
    spot = place.reshape(1)
    points = samples.shape[2]
    rows = gram_index.shape[0] // LANES
    tables = segment_tables(devices, spot)
    tables, index, offset = lax.optimization_barrier(
        (tables, gram_index.reshape(rows, LANES), gram_offset.reshape(rows, LANES))
    )
    weights = gram_tables(index, offset)
    tables, weights = lax.optimization_barrier((tables, weights))
    parts = segment_transform(samples.reshape(2, points // LANES, LANES), tables)
    received = lax.all_to_all(parts.reshape(devices, 16, LANES), AXES, 0, 0, tiled=True)
    real = device_transform(devices, received.reshape(16 * devices, LANES))
    timed = lax.all_to_all(real.reshape(-1), AXES, 0, 0, tiled=True)
    z_field, gram = times_block(
        devices, spot, timed.reshape(ROWS * devices, LANES), weights
    )
    return z_field.reshape(points), gram.reshape(-1)


def solution(mesh):
    return jax.shard_map(
        local,
        mesh=mesh,
        in_specs=(P(None, AXES, None), P(AXES), P(AXES)),
        out_specs=(P(AXES), P(AXES)),
        check_vma=False,
    )
```

```python
import functools
import math

import jax
import jax.numpy as jnp
import numpy as np
from jax import lax
from jax.experimental import pallas as pl
from jax.experimental.pallas import tpu as pltpu
from jax.sharding import PartitionSpec as P

GAP = 8
HALF = 16
UPS = 32
RATE = 4.0
SPREAD = HALF / 2.0
SIDE = 512
LANES = 128
KEPT = 5
ROWS = 9
AXES = ("inner", "outer")
F32 = jnp.float32
BF16 = jnp.bfloat16
MIB = 1 << 20


def halves(table):
    high = table.astype(jnp.bfloat16)
    low = (table - high.astype(np.float64)).astype(jnp.bfloat16)
    return np.stack([high, low])


def device_table(devices):
    n = np.arange(devices // 2)
    tables = []
    for g in range(2):
        angle = 2.0 * np.pi * ((2 * n[:, None] + g) * n[None, :] % devices) / devices
        tables.append(np.concatenate([np.cos(angle), np.sin(angle)], axis=1))
    return halves(np.stack(tables))


def split(x):
    high = x.astype(BF16)
    return high, (x - high.astype(F32)).astype(BF16)


def dot(a, b, dims):
    return lax.dot_general(a, b, (dims, ((), ())), preferred_element_type=F32)


def dot3(a, b, dims=((1,), (0,))):
    (a_high, a_low), (b_high, b_low) = a, b
    return dot(a_high, b_high, dims) + (dot(a_high, b_low, dims) + dot(a_low, b_high, dims))


def quarter(parts):
    (r0, i0), (r1, i1), (r2, i2), (r3, i3) = parts
    ar, ai, br, bi = r0 + r2, i0 + i2, r0 - r2, i0 - i2
    cr, ci, er, ei = r1 + r3, i1 + i3, r1 - r3, i1 - i3
    return [(ar + cr, ai + ci), (br + ei, bi - er), (ar - cr, ai - ci), (br - ei, bi + er)]


def times(a, b):
    return a[0] * b[0] - a[1] * b[1], a[0] * b[1] + a[1] * b[0]


def unit(count, period):
    half = period // 2
    near = ((count + half) & (period - 1)) - half
    angle = near.astype(F32) * (0.5 * math.pi / period)
    square = angle * angle
    sine, cosine = 1.0, 1.0
    for n in (4, 3, 2, 1):
        sine = 1.0 - square * (1.0 / ((2 * n) * (2 * n + 1))) * sine
    for n in (5, 4, 3, 2, 1):
        cosine = 1.0 - square * (1.0 / ((2 * n - 1) * (2 * n))) * cosine
    sine = angle * sine
    for _ in range(2):
        sine, cosine = 2.0 * sine * cosine, 1.0 - 2.0 * sine * sine
    return cosine, -sine


def segment_tables_kernel(devices, place_ref, table_ref, twiddle_ref, turn_ref):
    place = place_ref[0]
    points = SIDE * SIDE
    row = lax.broadcasted_iota(jnp.int32, (LANES, LANES), 0)
    lane = lax.broadcasted_iota(jnp.int32, (LANES, LANES), 1)
    line = lax.broadcasted_iota(jnp.int32, (8, LANES), 1)
    whole = unit(row * lane, LANES)
    across = times(unit(row * lane, points // 4), unit(place * row * 4, points * devices))
    down = unit(row, SIDE)
    for g in range(4):
        here = whole
        if g:
            here = times(whole, tuple(x[:1] for x in unit(line * g, SIDE)))
        (cos_high, cos_low), (sin_high, sin_low) = split(here[0]), split(-here[1])
        for k, (cos, sin) in enumerate(((cos_high, sin_high), (cos_low, sin_low))):
            table_ref[k, g, :LANES, :LANES] = cos
            table_ref[k, g, :LANES, LANES:] = sin
            table_ref[k, g, LANES:, :LANES] = -sin
            table_ref[k, g, LANES:, LANES:] = cos
        both = across
        step = down
        if g:
            part_g = times(unit(line * g, points), unit(place * g + 0 * line, points * devices))
            both = times(both, tuple(x[:1] for x in part_g))
            angle = -2.0 * math.pi * g * LANES / points
            step = times(down, (math.cos(angle), math.sin(angle)))
        for j in range(4):
            if j:
                both = times(both, step)
            for part in range(2):
                twiddle_ref[part, g, j] = both[part]
        turn = unit(place * (4 * line + g), SIDE * devices)
        for part in range(2):
            turn_ref[part, g] = turn[part]


def segment_kernel(x_ref, table_ref, twiddle_ref, turn_ref, out_ref, first_ref, second_ref):
    for j in range(4):
        grid = [
            tuple(x_ref[part, pl.ds(SIDE * i + j, LANES, stride=4), :] for part in range(2))
            for i in range(4)
        ]
        for g, pair in enumerate(quarter(grid)):
            for part in range(2):
                high, low = split(pair[part])
                rows, cols = pl.ds(LANES * part, LANES), pl.ds(LANES * j, LANES)
                first_ref[0, g, rows, cols] = high
                first_ref[1, g, rows, cols] = low
    for g in range(4):
        done = dot3((table_ref[0, g], table_ref[1, g]), (first_ref[0, g], first_ref[1, g]))
        grid = []
        for j in range(4):
            cols = slice(LANES * j, LANES * (j + 1))
            both = (twiddle_ref[0, g, j], twiddle_ref[1, g, j])
            grid.append(times((done[:LANES, cols], done[LANES:, cols]), both))
        for h, pair in enumerate(quarter(grid)):
            for part in range(2):
                high, low = split(pair[part])
                rows, cols = pl.ds(LANES * g, LANES), pl.ds(LANES * part, LANES)
                second_ref[0, h, rows, cols] = high
                second_ref[1, h, rows, cols] = low
    for h in range(4):
        done = dot3(
            (second_ref[0, h], second_ref[1, h]), (table_ref[0, h], table_ref[1, h]), ((1,), (1,))
        )
        pair = times((done[:, :LANES], done[:, LANES:]), (turn_ref[0, h, :1], turn_ref[1, h, :1]))
        for part in range(2):
            for upper in range(2):
                out_ref[pl.ds(8 * part + 4 * upper + h, SIDE // 2, stride=16), :] = pair[part][
                    SIDE // 2 * upper : SIDE // 2 * (upper + 1)
                ]


def device_kernel(devices, x_ref, table_ref, out_ref):
    count = devices // 2
    edges = {}
    for block in range(4):
        columns = ([], [])
        for e in (2 * block, 2 * block + 1):
            pairs = [
                [x_ref[pl.ds(16 * count * i + 8 * part + e, count, stride=16), :] for i in range(2)]
                for part in range(2)
            ]
            columns[0].append(jnp.concatenate([low + high for low, high in pairs], axis=0))
            columns[1].append(jnp.concatenate([low - high for low, high in pairs], axis=0))
        for g in range(2):
            x = jnp.concatenate(columns[g], axis=1)
            done = dot3((table_ref[0, g], table_ref[1, g]), split(x))
            for i, e in enumerate((2 * block, 2 * block + 1)):
                values = done[:, LANES * i : LANES * (i + 1)]
                out_ref[pl.ds(ROWS * g + e, count, stride=2 * ROWS), :] = values
                if e % 4 in (0, 3):
                    edges[e, g] = values
    lane = lax.broadcasted_iota(jnp.int32, (count, LANES), 1)
    row = lax.broadcasted_iota(jnp.int32, (count, LANES), 0)
    after, before = [], []
    for g in range(2):
        after.append(jnp.where(lane == 0, edges[0, g], pltpu.roll(edges[4, g], 1, 1)))
        before.append(
            jnp.where(lane == LANES - 1, edges[3, g], pltpu.roll(edges[7, g], LANES - 1, 1))
        )
    later = jnp.where(row == count - 1, 0.0, pltpu.roll(after[0], count - 1, 0))
    earlier = jnp.where(row == 0, 0.0, pltpu.roll(before[1], 1, 0))
    for g, (up, down) in enumerate(((after[1], earlier), (later, before[0]))):
        out_ref[pl.ds(ROWS * g + 8, count, stride=2 * ROWS), :] = jnp.where(lane < 2, up, down)


def gain(devices, place, position):
    length = SIDE * SIDE * devices
    centred = place.astype(F32) / devices + position.astype(F32) / length - 0.5
    return length ** (-0.5) * jnp.exp(RATE * centred * centred)


def gram_tables_kernel(index_ref, offset_ref, code_ref, share_ref, entry_ref):
    for odd in range(2):
        rows = pl.ds(odd, LANES, stride=2)
        code = (offset_ref[rows, :] * GAP + index_ref[rows, :]).T
        code_ref[odd] = code
        fraction = (code >> 3).astype(F32) * (1.0 / UPS)
        for w, share in enumerate(shares_of(fraction)[:KEPT]):
            share_ref[w, odd] = share
    line = lax.broadcasted_iota(jnp.int32, (8, LANES), 1) & (UPS - 1)
    for w, share in enumerate(shares_of(line.astype(F32) * (1.0 / UPS))[KEPT:]):
        entry_ref[w] = share


def shares_of(fraction):
    sine = jnp.sin(math.pi * fraction) * (1.0 / math.pi)
    sine = sine * jnp.exp(fraction * fraction * (-0.5 / (SPREAD * SPREAD)))
    at_zero = fraction == 0.0
    shares = [jnp.where(at_zero, 1.0, sine / jnp.where(at_zero, 1.0, fraction))]
    square = fraction * fraction
    up = jnp.exp(fraction * (1.0 / (SPREAD * SPREAD)))
    for w in range(1, HALF, 2):
        odd, even = square - w * w, square - (w + 1) * (w + 1)
        inverse = 1.0 / (odd * even)
        for tap, other in ((w, even), (w + 1, odd)):
            scale = (-1.0) ** tap * math.exp(-0.5 * tap * tap / (SPREAD * SPREAD))
            sine = sine * up
            shares.append((sine * scale) * (other * inverse))
    shares.append(jnp.exp(fraction * (-2.0 / (SPREAD * SPREAD))))
    return shares


def weighted(taps, shares, fraction):
    down = shares[HALF + 1]
    downs = down
    terms = [taps[HALF - 1] * shares[0]]
    for w in range(1, HALF + 1):
        term = taps[HALF - 1 + w] * (fraction + w)
        if w < HALF:
            term = term + (downs * taps[HALF - 1 - w]) * (fraction - w)
        terms.append(term * shares[w])
        downs = downs * down
    while len(terms) > 1:
        terms = [a + b for a, b in zip(terms[::2], terms[1::2])] + terms[len(terms) & ~1 :]
    return terms[0]


def times_kernel(
    devices, place_ref, x_ref, code_ref, share_ref, entry_ref, z_hbm, gram_hbm,
    zs_ref, z_ref, ends_ref, sums, gram_ref, sem, gram_sem,
):
    pad = HALF
    place = place_ref[0]
    length = SIDE * SIDE * devices
    t = lax.broadcasted_iota(jnp.int32, (LANES, LANES), 0)
    line = lax.broadcasted_iota(jnp.int32, (8, LANES), 1)
    for h in range(4):
        begin = SIDE * (4 * line + h)
        base = gain(devices, place, begin)[:1]
        start_c = (place.astype(F32) / devices + begin.astype(F32) / length - 0.5)[:1]
        for g in range(4):
            start = ROWS * LANES * (g % 2) + 4 * (g // 2) + h
            raw = x_ref[pl.ds(start, LANES, stride=ROWS), :]
            du = (4 * t + g).astype(F32) * (1.0 / length)
            x = (du * (2.0 * RATE)) * (start_c + 0.5 * du)
            factor = base + base * (x + 0.5 * x * x)
            zs_ref[h, pl.ds(pad + g, LANES, stride=4), :] = raw * factor
        for block in range(4):
            z_ref[pl.ds(4 * h + block, LANES, stride=16), :] = zs_ref[
                h, pl.ds(pad + LANES * block, LANES), :
            ].T
    copy = pltpu.make_async_copy(z_ref, z_hbm, sem)
    copy.start()
    for g in range(4):
        upper = g // 2
        for side, top, shift in ((0, LANES - 8, 1 + upper), (1, 0, LANES - 1 - upper)):
            start = ROWS * (LANES * (g % 2) + top) + 8
            tile = pltpu.roll(x_ref[pl.ds(start, 8, stride=ROWS), :], shift, 1)
            ends_ref[side, pl.ds(g, 8, stride=4), :] = tile
    lane = lax.broadcasted_iota(jnp.int32, (pad, LANES), 1)
    for h in range(4):
        before = zs_ref[(h - 1) % 4, pl.ds(SIDE, pad), :]
        after = zs_ref[(h + 1) % 4, pl.ds(pad, pad), :]
        if h == 0:
            edge = ends_ref[0, pl.ds(pad, pad), :] * gain(
                devices, place - 1, t[:pad] + (SIDE * SIDE - HALF)
            )
            before = jnp.where(lane == 0, edge, pltpu.roll(before, 1, 1))
        if h == 3:
            edge = ends_ref[1, pl.ds(0, pad), :] * gain(devices, place + 1, t[:pad])
            after = jnp.where(lane == LANES - 1, edge, pltpu.roll(after, LANES - 1, 1))
        zs_ref[h, pl.ds(0, pad), :] = before
        zs_ref[h, pl.ds(pad + SIDE, pad), :] = after
    for h in range(4):

        def body(step, carry, h=h):
            rows = pl.ds(pl.multiple_of(64 * (h % 2) + 8 * step, 8), 8)
            index = code_ref[h // 2, rows, :]
            offset = index >> 3
            fraction = offset.astype(F32) * (1.0 / UPS)
            taps = [
                zs_ref[h, pl.ds(pad + o + 64 * step, 8, stride=8), :]
                for o in range(1 - HALF, HALF + GAP)
            ]
            for bit in (2, 1, 0):
                size = 1 << bit
                chosen = (index >> bit & 1) == 1
                taps = [jnp.where(chosen, b, a) for a, b in zip(taps[:-size], taps[size:])]
            shares = [share_ref[w, h // 2, rows, :] for w in range(KEPT)]
            for w in range(HALF + 2 - KEPT):
                shares.append(jnp.take_along_axis(entry_ref[w], offset, axis=1))
            sums[h // 2, rows, :] = weighted(taps, shares, fraction)
            return carry

        lax.fori_loop(0, 8, body, 0, unroll=4)
    for odd in range(2):
        gram_ref[pl.ds(odd, LANES, stride=2), :] = sums[odd].T
    gram_copy = pltpu.make_async_copy(gram_ref, gram_hbm, gram_sem)
    gram_copy.start()
    copy.wait()
    gram_copy.wait()


def call(kernel, out_shape, specs, scratch=(), flops=0, limit=16, outs="v"):
    spaces = {"s": pltpu.SMEM, "v": pltpu.VMEM, "h": pltpu.HBM}
    out_specs = [pl.BlockSpec(memory_space=spaces[spec]) for spec in outs]
    if len(outs) == 1:
        out_specs = out_specs[0]
    return pl.pallas_call(
        kernel,
        out_shape=out_shape,
        in_specs=[pl.BlockSpec(memory_space=spaces[spec]) for spec in specs],
        out_specs=out_specs,
        scratch_shapes=list(scratch),
        compiler_params=pltpu.CompilerParams(vmem_limit_bytes=limit * MIB),
        cost_estimate=pl.CostEstimate(flops=flops, bytes_accessed=4 * MIB, transcendentals=0),
    )


def struct(shape, kind=F32):
    return jax.ShapeDtypeStruct(tuple(shape), kind)


def segment_tables(devices, place):
    return call(
        functools.partial(segment_tables_kernel, devices),
        (
            struct((2, 4, 2 * LANES, 2 * LANES), BF16),
            struct((2, 4, 4, LANES, LANES)),
            struct((2, 4, 8, LANES)),
        ),
        "s",
        flops=1 << 32,
        outs="vvv",
    )(place)


def segment_transform(samples, tables):
    points = samples.size // 2
    return call(
        segment_kernel,
        struct((points * 2 // LANES, LANES)),
        "vvvv",
        [
            pltpu.VMEM((2, 4, 2 * LANES, SIDE), BF16),
            pltpu.VMEM((2, 4, SIDE, 2 * LANES), BF16),
        ],
        3 * 2 * 8 * SIDE * SIDE * LANES,
    )(samples, *tables)


def device_transform(devices, received):
    return call(
        functools.partial(device_kernel, devices),
        struct((ROWS * devices, LANES)),
        "vv",
        flops=3 * 2 * 2 * devices * received.shape[0] // 2 * LANES,
    )(received, jnp.asarray(device_table(devices)))


def gram_tables(index, offset):
    square = (2, LANES, LANES)
    return call(
        gram_tables_kernel,
        (
            struct(square, jnp.int32),
            struct((KEPT,) + square),
            struct((HALF + 2 - KEPT, 8, LANES)),
        ),
        "vv",
        flops=1 << 26,
        outs="vvv",
    )(index, offset)


def times_block(devices, place, timed, tables):
    rows = SIDE * SIDE // LANES
    return call(
        functools.partial(times_kernel, devices),
        (struct((rows, LANES)), struct((2 * LANES, LANES))),
        "svvvv",
        [
            pltpu.VMEM((4, SIDE + 2 * HALF, LANES), F32),
            pltpu.VMEM((rows, LANES), F32),
            pltpu.VMEM((2, 2 * HALF, LANES), F32),
            pltpu.VMEM((2, LANES, LANES), F32),
            pltpu.VMEM((2 * LANES, LANES), F32),
            pltpu.SemaphoreType.DMA(()),
            pltpu.SemaphoreType.DMA(()),
        ],
        1 << 24,
        outs="hh",
    )(place, timed, *tables)


def local(samples, gram_index, gram_offset):
    inner, outer = lax.axis_size("inner"), lax.axis_size("outer")
    devices = inner * outer
    place = (lax.axis_index("inner") * outer + lax.axis_index("outer")).astype(jnp.int32)
    spot = place.reshape(1)
    points = samples.shape[2]
    rows = gram_index.shape[0] // LANES
    tables = segment_tables(devices, spot)
    tables, index, offset = lax.optimization_barrier(
        (tables, gram_index.reshape(rows, LANES), gram_offset.reshape(rows, LANES))
    )
    weights = gram_tables(index, offset)
    tables, weights = lax.optimization_barrier((tables, weights))
    parts = segment_transform(samples.reshape(2, points // LANES, LANES), tables)
    received = lax.all_to_all(parts.reshape(devices, 16, LANES), AXES, 0, 0, tiled=True)
    real = device_transform(devices, received.reshape(16 * devices, LANES))
    timed = lax.all_to_all(real.reshape(-1), AXES, 0, 0, tiled=True)
    z_field, gram = times_block(
        devices, spot, timed.reshape(ROWS * devices, LANES), weights
    )
    return z_field.reshape(points), gram.reshape(-1)


def solution(mesh):
    return jax.shard_map(
        local,
        mesh=mesh,
        in_specs=(P(None, AXES, None), P(AXES), P(AXES)),
        out_specs=(P(AXES), P(AXES)),
        check_vma=False,
    )
```
